512 devices in a mesh: member: 16 (over z, x_hi), lat: 32 (over x_lo, y, core).
Axes of the slice: x: 4 (x_hi: 2, x_lo: 2; x = x_hi * 2 + x_lo), y: 8, z: 8, core: 2. Of those that a mesh axis runs over, the one named last changes fastest.
Arguments:
- state: bfloat16 [16, 64, 2, 256, 1024], P('member', None, None, 'lat'), may hold values from -6 to 6
- target: bfloat16 [2, 64, 256, 256], P(None, None, 'lat'), may hold values from -6 to 6
- w_in: bfloat16 [64, 256], replicated, may hold values from -0.75 to 0.75
- w_out: bfloat16 [256, 64], replicated, may hold values from -0.375 to 0.375
- legendre: bfloat16 [256, 256, 256], P('lat'), may hold values from -0.25 to 0.25
- wavenumber_of: int32 [256], replicated, may hold values from 0 to 255, each once
Outputs:
- loss_mean: float32 [], replicated
- grad_w_in: float32 [64, 256], replicated
- grad_w_out: float32 [256, 64], replicated
The draws below stay inside these ranges and needn't reach their ends.
Inputs may be any that keep to these rules, and one draw needn't show every extreme that they name: `wavenumber_of`: a permutation of the wavenumbers 0 to 256 - 1 over the slots.
All inputs are finite; a program needn't handle non-finite values.
Results may differ from the reference program's by a relative error of at most 0.0055.
Values may be sent and summed in bfloat16 or wider, within the bound.
A program may use at most 64 MiB of HBM per device.

```python
import math
import jax
import jax.numpy as jnp
from jax import lax

C = 64
HID = 256
NLON = 1024
M = 256
N = 256
NHALF = 256
MEMBERS = 16


def steps_of(own_key, dims, shards, least, high):
    loudness, own = 1.0, jax.random.fold_in(own_key, 6)
    for axis_at, parts in shards:
        draws = jnp.exp(jax.random.uniform(jax.random.fold_in(own, axis_at), (parts,), jnp.float32, least / len(shards), high / len(shards)))
        loudness = loudness * jnp.repeat(draws, dims[axis_at] // parts).reshape([-1 if axis == axis_at else 1 for axis in range(len(dims))])
    return loudness


def noise(own_key, shape, scale, limit, cuts=(), kind=jnp.bfloat16):
    gain = steps_of(own_key, shape, cuts, -0.22, 0.18) if cuts else 1.0
    array = jax.random.normal(own_key, shape, jnp.float32) * scale * gain
    return jnp.minimum(jnp.maximum(array, -limit), limit).astype(kind)


def setup_inputs(seed: int = 0) -> dict:
    seeds = jax.random.split(jax.random.key(seed), 7)
    state = noise(seeds[0], (MEMBERS, C, 2, NHALF, NLON), 1.0, 6.0, ((0, 16), (3, 32)))
    target = noise(seeds[1], (2, C, M, N), 1.0, 6.0, ((2, 32),))
    w_in = noise(seeds[2], (C, HID), C ** -0.5, 0.75)
    w_out = noise(seeds[3], (HID, C), HID ** -0.5, 0.375)
    legendre = noise(seeds[4], (M, N, NHALF), (2 * NHALF) ** -0.5, 0.25, ((0, 32),))
    wavenumber_of = jax.random.permutation(seeds[5], M).astype(jnp.int32)
    return dict(state=state, target=target, w_in=w_in, w_out=w_out, legendre=legendre, wavenumber_of=wavenumber_of)


def make_waves(longitude_count, wavenumber_of, slot_count, lane_count):
    slot_waves = wavenumber_of.reshape(lane_count, 1, slot_count)
    col_waves = jnp.broadcast_to(slot_waves, (lane_count, 2, slot_count)).reshape(-1)
    col_part = jnp.broadcast_to(jnp.arange(2, dtype=jnp.int32).reshape(1, 2, 1), (lane_count, 2, slot_count)).reshape(-1)
    longitude_cells = jnp.arange(longitude_count, dtype=jnp.int32)
    phase_index = longitude_cells[:, None] * col_waves[None, :] % longitude_count
    angle_rad = phase_index.astype(jnp.float32) * (2.0 * math.pi / longitude_count)
    values = jnp.where(col_part[None, :] == 0, jnp.cos(angle_rad), -jnp.sin(angle_rad)) / math.sqrt(longitude_count)
    return values.astype(jnp.bfloat16)

def smooth_abs(delta):
    return jnp.sqrt(delta * delta + 1.0) - 1.0

def smooth_slope(delta):
    return delta / jnp.sqrt(delta * delta + 1.0)

def silu_grad(pre_act):
    sigma_value = jax.nn.sigmoid(pre_act)
    return sigma_value * (1.0 + pre_act * (1.0 - sigma_value))

def reference(state, target, w_in, w_out, legendre, wavenumber_of):
    members, channels, hemi_count, half_rows, longitude_count = state.shape
    wave_count, degrees = (legendre.shape[0], legendre.shape[1])
    groups = members // 2
    obj_scale = 1.0 / (groups * channels)
    wavenumber_lookup = make_waves(longitude_count, wavenumber_of, wave_count, 1)
    legendre_wide = legendre.astype(jnp.float32)
    degree = jnp.arange(degrees, dtype=jnp.int32)
    degree_gap = degree[None, :] - wavenumber_of[:, None]
    live_mask = (degree_gap >= 0).astype(jnp.float32)
    sign_south = (1 - 2 * (degree_gap % 2)).astype(jnp.float32)
    target_wide = target.astype(jnp.float32)

    def forward(member_field):
        flattened_state = member_field.reshape(channels, -1)
        pre_act = jnp.dot(w_in.T, flattened_state, preferred_element_type=jnp.float32)
        hidden = jax.nn.silu(pre_act).astype(jnp.bfloat16)
        tendency_field = jnp.dot(w_out.T, hidden, preferred_element_type=jnp.float32)
        predicted_field = (flattened_state.astype(jnp.float32) + tendency_field).astype(jnp.bfloat16)
        fourier_modes = jnp.dot(predicted_field.reshape(-1, longitude_count), wavenumber_lookup, preferred_element_type=jnp.float32)
        fourier_modes = fourier_modes.astype(jnp.bfloat16).reshape(channels, 2, half_rows, 2, wave_count)
        hemi_sums = jnp.einsum('chiqs,sni->hqcsn', fourier_modes.astype(jnp.float32), legendre_wide)
        coeffs = ((hemi_sums[0] + sign_south * hemi_sums[1]) * live_mask).astype(jnp.bfloat16)
        return (flattened_state, pre_act, hidden, coeffs)

    def backward(flattened_state, pre_act, hidden, coef_grad):
        south_grad = coef_grad * sign_south.astype(jnp.bfloat16)
        stacked = jnp.stack([coef_grad, south_grad]).astype(jnp.float32)
        back_fourier = jnp.einsum('hqcsn,sni->chiqs', stacked, legendre_wide).astype(jnp.bfloat16)
        back_fourier = back_fourier.reshape(-1, 2 * wave_count)
        grid_part = jnp.dot(back_fourier, wavenumber_lookup.T, preferred_element_type=jnp.float32)
        flat_grad = grid_part.astype(jnp.bfloat16).reshape(channels, -1)
        grad_out = jnp.dot(hidden, flat_grad.T, preferred_element_type=jnp.float32)
        hidden_pull = jnp.dot(w_out, flat_grad, preferred_element_type=jnp.float32)
        act_grad = (hidden_pull * silu_grad(pre_act)).astype(jnp.bfloat16)
        grad_in = jnp.dot(flattened_state, act_grad.T, preferred_element_type=jnp.float32)
        return (grad_in, grad_out)

    def member_terms(own_out, mate_coeffs):
        flattened_state, pre_act, hidden, coeffs = own_out
        own_values = coeffs.astype(jnp.float32)
        misfit = own_values - target_wide
        spread = own_values - mate_coeffs.astype(jnp.float32)
        share_part = jnp.sum(live_mask * (0.5 * smooth_abs(misfit) - 0.25 * smooth_abs(spread)))
        coef_grad = (live_mask * (0.5 * smooth_slope(misfit) - 0.5 * smooth_slope(spread)) * obj_scale).astype(jnp.bfloat16)
        grad_in, grad_out = backward(flattened_state, pre_act, hidden, coef_grad)
        return (grad_in, grad_out, share_part)

    def one_group(pair_fields):
        leading_output = forward(pair_fields[0])
        second_out = forward(pair_fields[1])
        in_a, out_a, part_a = member_terms(leading_output, second_out[3])
        in_b, out_b, part_b = member_terms(second_out, leading_output[3])
        return (in_a + in_b, out_a + out_b, part_a + part_b)
    paired = state.reshape(groups, 2, channels, hemi_count, half_rows, longitude_count)
    grad_ins, grad_outs, shares = lax.map(one_group, paired)
    total = jnp.sum(shares)
    loss_mean = total * obj_scale / (wave_count * degrees)
    return (loss_mean, lax.optimization_barrier(jnp.sum(grad_ins, axis=0)), lax.optimization_barrier(jnp.sum(grad_outs, axis=0)))
```

```python
import functools
import math

import jax
import jax.numpy as jnp
import numpy as np
from jax import lax
from jax.experimental import pallas as pl
from jax.experimental.pallas import tpu as pltpu
from jax.sharding import PartitionSpec as P

MESH = pl.DeviceIdType.MESH
F32 = jnp.float32
BF16 = jnp.bfloat16
XC = 256
JP = 4


def dot(a, b):
    return jnp.dot(a, b, preferred_element_type=F32)


def base_table(nlon, waves):
    cell = np.arange(nlon, dtype=np.int64)[None, :]
    wave = np.arange(waves, dtype=np.int64)[:, None]
    angle = (cell * wave % nlon).astype(np.float32) * np.float32(2.0 * math.pi / nlon)
    both = np.concatenate([np.cos(angle), -np.sin(angle)], axis=0) / np.float32(math.sqrt(nlon))
    return both.astype(jnp.bfloat16)


def kernel(
    nm, nl, state_hbm, target_hbm, w_in_ref, w_out_ref, leg_hbm, base_hbm, wcol_ref,
    out_in, out_out, out_loss,
    st_raw, st32, s_cx, base, wave_t, wave, w_in_bd, w_out_bd, w_pull, hid, slope, fore,
    sf, rf, rf32, fg32, sg, rg, leg, leg_t, tgt, tw, tgt_t, acc32, gb, bs, acc,
    lsend, lrow1, lsend2, lrow2, ar_s, ar_a, ar_p, ar_b, ar_q, ar_c,
    in_sem, send1, recv1, send2, recv2, ls_sem, lr_sem, as_sem, arr_sem,
):
    member = lax.axis_index("member")
    lat = lax.axis_index("lat")
    half = lax.rem(member, 2)
    base_member = member - half
    ng = 2 * nl
    me = half * nl + lat
    nlon = wave.shape[0]
    cols = wave.shape[1]
    waves = cols // 2
    deg = leg.shape[1]
    nj = leg.shape[2]

    def at64(t):
        return (base_member + t // nl, lax.rem(t, nl))

    c_state = pltpu.make_async_copy(state_hbm, st_raw, in_sem.at[0])
    c_base = pltpu.make_async_copy(base_hbm, base, in_sem.at[1])
    c_leg = pltpu.make_async_copy(leg_hbm.at[pl.ds(half * 4, 4)], leg, in_sem.at[2])
    c_tgt = pltpu.make_async_copy(target_hbm, tgt, in_sem.at[3])
    c_state.start()
    c_base.start()
    c_leg.start()
    c_tgt.start()

    barrier = pltpu.get_barrier_semaphore()

    def greet(d, carry):
        pl.semaphore_signal(barrier, inc=1, device_id=at64(lax.rem(me + d, ng)), device_id_type=MESH)
        return carry

    lax.fori_loop(1, ng, greet, 0)

    def greet_member(d, carry):
        other = lax.rem(base_member + d, nm)
        pl.semaphore_signal(barrier, inc=1, device_id=(other, lat), device_id_type=MESH)
        return carry

    lax.fori_loop(2, nm, greet_member, 0)

    w_in_bd[...] = jnp.zeros_like(w_in_bd)
    w_pull[...] = jnp.zeros_like(w_pull)
    wide = w_out_ref[...].astype(F32)
    wide = jnp.concatenate([wide, wide, wide, wide], axis=1)
    wide_t = wide.T.astype(BF16)
    lane_group = lax.broadcasted_iota(jnp.int32, wide.shape, 1) >> 6
    for g in range(4):
        w_in_bd[64 * g : 64 * g + 64, 256 * g : 256 * g + 256] = w_in_ref[...]
        w_pull[64 * g : 64 * g + 64, 256 * g : 256 * g + 256] = wide_t[64 * g : 64 * g + 64]
        w_out_bd[256 * g : 256 * g + 256, :] = jnp.where(lane_group == g, wide, 0.0).astype(BF16)

    c_state.wait()

    def widen(xt, carry):
        lanes = pl.ds(pl.multiple_of(xt * 128, 128), 128)
        st32[xt] = st_raw[:, :, :, lanes].astype(F32).reshape(st32.shape[1], 128)
        return carry

    lax.fori_loop(0, nlon // 128, widen, 0)

    c_base.wait()
    lb = min(128, waves)
    rb = min(128, cols)

    def order_rows(r, carry):
        rows = pl.ds(pl.multiple_of(r * rb, rb), rb)
        wcol = wcol_ref[rows, :][:, :lb]
        part = (lax.broadcasted_iota(jnp.int32, (rb, lb), 0) >> 2) & 1
        lane = lax.broadcasted_iota(jnp.int32, (rb, lb), 1)
        blocks = []
        for b in range(cols // lb):
            q, first = b * lb // waves, b * lb % waves
            hit = jnp.where(wcol == lane + first, 1.0, 0.0) * jnp.where(part == q, 1.0, 0.0)
            blocks.append(hit)
        pick = jnp.concatenate(blocks, axis=1).astype(BF16)
        wave_t[rows, :] = dot(pick, base[...]).astype(BF16)
        return carry

    lax.fori_loop(0, cols // rb, order_rows, 0)

    def send_chunk(jp, src, dst, ssem, rsem):
        def one(d, carry):
            t = lax.rem(me + d, ng)
            pltpu.make_async_remote_copy(
                src_ref=src.at[jp, t], dst_ref=dst.at[jp, me],
                send_sem=ssem.at[jp], recv_sem=rsem.at[jp],
                device_id=at64(t), device_id_type=MESH,
            ).start()
            return carry

        lax.fori_loop(1, ng, one, 0)

    def wait_bytes(ref, sem):
        pltpu.make_async_copy(ref, ref, sem).wait()

    def forward(jp, carry):
        def network(xc, inner):
            rows = pl.ds(pl.multiple_of(xc * XC, XC), XC)
            turned = []
            for xt in range(XC // 128):
                tile = xc * (XC // 128) + xt
                parts = [
                    st32[tile, pl.ds(h * 8 + jp * 2 + j2, 64, stride=16), :]
                    for j2 in range(2) for h in range(2)
                ]
                block = jnp.concatenate(parts, axis=0)
                s_cx[jp, :, pl.ds(pl.multiple_of(tile * 128, 128), 128)] = block.astype(BF16)
                turned.append(block.T)
            field = jnp.concatenate(turned, axis=0)
            pre = dot(field.astype(BF16), w_in_bd[...])
            sig = 0.5 + 0.5 * jnp.tanh(0.5 * pre)
            hidden = (pre * sig).astype(BF16)
            hid[jp, rows, :] = hidden
            slope[jp, rows, :] = (sig * (1.0 + pre * (1.0 - sig))).astype(BF16)
            fore[rows, :] = (field + dot(hidden, w_out_bd[...])).astype(BF16)
            return inner

        lax.fori_loop(0, nlon // XC, network, 0)
        modes = dot(wave_t[...], fore[...])
        pair = [modes[:, :128].reshape(ng, 8, 128), modes[:, 128:].reshape(ng, 8, 128)]
        sf[jp] = jnp.concatenate(pair, axis=1).astype(BF16)

        @pl.when(jp == 0)
        def _():
            pl.semaphore_wait(barrier, ng - 1 + nm - 2)

        send_chunk(jp, sf, rf, send1, recv1)
        rf[jp, me] = sf[jp, me]
        return carry

    lax.fori_loop(0, JP, forward, 0)

    def turn_wave(xt, carry):
        start = pl.multiple_of(xt * 128, 128)
        wave[pl.ds(start, 128), :] = wave_t[:, pl.ds(start, 128)].astype(F32).T.astype(BF16)
        return carry

    lax.fori_loop(0, nlon // 128, turn_wave, 0)
    c_leg.wait()
    c_tgt.wait()
    for i in range(4):
        leg_t[i] = leg[i].astype(F32).T.astype(BF16)
    for b in range(deg // 128):
        tw[b] = tgt[:, :, :, 128 * b : 128 * b + 128].astype(F32).reshape(tw.shape[1], 128)
    for b in range(deg // 128):
        for i in range(8):
            parts = [tw[b, pl.ds(q * 512 + i, 64, stride=8), :] for q in (0, 0, 1, 1)]
            tgt_t[i, 128 * b : 128 * b + 128, :] = jnp.concatenate(parts, axis=0).T.astype(BF16)

    def arrived(jp, carry):
        wait_bytes(rf.at[jp, pl.ds(0, ng - 1)], recv1.at[jp])
        rf32[:, pl.ds(pl.multiple_of(jp * 16, 16), 16), :] = rf[jp].astype(F32)
        return carry

    lax.fori_loop(0, JP, arrived, 0)

    for i in range(4):
        for e in range(2):
            parts = [
                rf32[e * nl : e * nl + nl, pl.ds(q * 4 + i, 8, stride=8), :].reshape(nj, 128)
                for q in range(2)
            ]
            acc32[i, e] = dot(leg[i], jnp.concatenate(parts, axis=1).astype(BF16))

    own = wcol_ref[pl.ds(pl.multiple_of(me * 8, 8), 8), :]
    obj = 1.0 / ((nm // 2) * 64)
    nb = 64

    def compare(c, carry):
        rows = pl.ds(pl.multiple_of(c * nb, nb), nb)
        degree = lax.broadcasted_iota(jnp.int32, (nb, 128), 0) + c * nb
        south = lax.broadcasted_iota(jnp.int32, (nb, 128), 1) >= 64
        loss = jnp.zeros((nb, 128), F32)
        for i in range(4):
            gap = degree - own[i : i + 1, :]
            live = gap >= 0
            sign = jnp.where((gap & 1) == 0, 1.0, -1.0)
            turn = jnp.where(south, sign, 1.0)
            for q in range(2):
                lanes = slice(128 * q, 128 * q + 128)
                coeffs = []
                for e in range(2):
                    part = acc32[i, e, rows, lanes]
                    whole = part + sign * pltpu.roll(part, 64, axis=1)
                    coeffs.append(jnp.where(live, whole, 0.0).astype(BF16).astype(F32))
                aim = tgt_t[half * 4 + i, rows, lanes].astype(F32) * turn
                d0, d1, ds = coeffs[0] - aim, coeffs[1] - aim, coeffs[0] - coeffs[1]
                u0, u1, us = d0 * d0 + 1.0, d1 * d1 + 1.0, ds * ds + 1.0
                r0, r1, rs = lax.rsqrt(u0), lax.rsqrt(u1), lax.rsqrt(us)
                term = 0.5 * ((u0 * r0 - 1.0) + (u1 * r1 - 1.0) - (us * rs - 1.0))
                loss = loss + jnp.where(live, term, 0.0)
                slope_s = 0.5 * (ds * rs)
                gb[i, 0, rows, lanes] = jnp.where(live, (0.5 * (d0 * r0) - slope_s) * obj, 0.0).astype(BF16)
                gb[i, 1, rows, lanes] = jnp.where(live, (0.5 * (d1 * r1) + slope_s) * obj, 0.0).astype(BF16)
        return carry + jnp.sum(loss.reshape(nb // 8, 8, 128), axis=0)

    loss8 = lax.fori_loop(0, deg // nb, compare, jnp.zeros((8, 128), F32))

    for i in range(4):
        for e in range(2):
            back = dot(leg_t[i], gb[i, e])
            for q in range(2):
                fg32[e * nl : e * nl + nl, pl.ds(q * 4 + i, 8, stride=8), :] = back[
                    :, 128 * q : 128 * q + 128
                ].reshape(nl, 8, 128)

    def give_back(jp, carry):
        sg[jp] = fg32[:, pl.ds(pl.multiple_of(jp * 16, 16), 16), :].astype(BF16)
        send_chunk(jp, sg, rg, send2, recv2)
        rg[jp, me] = sg[jp, me]
        return carry

    lax.fori_loop(0, JP, give_back, 0)

    def to_lats(src_of, dst, ssem, rsem):
        def one(d, carry):
            t = lax.rem(lat + d, nl)
            pltpu.make_async_remote_copy(
                src_ref=src_of(t), dst_ref=dst.at[lat], send_sem=ssem, recv_sem=rsem,
                device_id=(member, t), device_id_type=MESH,
            ).start()
            return carry

        lax.fori_loop(1, nl, one, 0)

    def to_members(src, dst, ssem, rsem):
        def one(d, carry):
            t = lax.rem(member + d, nm)
            pltpu.make_async_remote_copy(
                src_ref=src, dst_ref=dst.at[member], send_sem=ssem, recv_sem=rsem,
                device_id=(t, lat), device_id_type=MESH,
            ).start()
            return carry

        lax.fori_loop(1, nm, one, 0)

    lsend[...] = jnp.sum(loss8, axis=0, keepdims=True)
    to_lats(lambda t: lsend, lrow1, ls_sem.at[0], lr_sem.at[0])
    lrow1[lat] = lsend[...]

    acc[...] = jnp.zeros_like(acc)

    def backward(jp, carry):
        wait_bytes(rg.at[jp, pl.ds(0, ng - 1)], recv2.at[jp])
        block = rg[jp].astype(F32)
        bs[:, :128] = block[:, :8].reshape(cols, 128).astype(BF16)
        bs[:, 128:] = block[:, 8:].reshape(cols, 128).astype(BF16)

        def network(xc, inner):
            rows = pl.ds(pl.multiple_of(xc * XC, XC), XC)
            grad = dot(wave[rows, :], bs[...]).astype(BF16)
            act = (dot(grad, w_pull[...]) * slope[jp, rows, :].astype(F32)).astype(BF16)
            turned = grad.astype(F32).T.astype(BF16)
            top = jnp.zeros((64, 256), F32)
            low = jnp.zeros((64, 256), F32)
            for g in range(4):
                lanes = slice(256 * g, 256 * g + 256)
                top = top + dot(turned[64 * g : 64 * g + 64], hid[jp, rows, lanes])
                low = low + dot(s_cx[jp, 64 * g : 64 * g + 64, rows], act[:, lanes])
            acc[:64] += top
            acc[64:] += low
            return inner

        lax.fori_loop(0, nlon // XC, network, 0)
        return carry

    lax.fori_loop(0, 1, backward, 0)
    wait_bytes(lrow1.at[pl.ds(0, nl - 1)], lr_sem.at[0])
    lsend2[...] = jnp.sum(lrow1[...], axis=0)
    to_members(lsend2, lrow2, ls_sem.at[1], lr_sem.at[1])
    lrow2[member] = lsend2[...]
    lax.fori_loop(1, JP, backward, 0)

    per = 32 // nl
    for t in range(32):
        r, c = t // 2, t % 2
        ar_s[t // per, 8 * (t % per) : 8 * (t % per) + 8, :] = acc[8 * r : 8 * r + 8, 128 * c : 128 * c + 128]
    to_lats(lambda t: ar_s.at[t], ar_a, as_sem.at[0], arr_sem.at[0])
    ar_a[lat] = ar_s[lat]
    wait_bytes(ar_a.at[pl.ds(0, nl - 1)], arr_sem.at[0])
    ar_p[...] = jnp.sum(ar_a[...], axis=0)
    to_members(ar_p, ar_b, as_sem.at[1], arr_sem.at[1])
    ar_b[member] = ar_p[...]
    wait_bytes(ar_b.at[pl.ds(0, nm - 1)], arr_sem.at[1])
    ar_q[...] = jnp.sum(ar_b[...], axis=0)
    to_lats(lambda t: ar_q, ar_c, as_sem.at[2], arr_sem.at[2])
    ar_c[lat] = ar_q[...]
    wait_bytes(lrow2.at[pl.ds(0, nm - 1)], lr_sem.at[1])
    out_loss[...] = jnp.sum(lrow2[...], axis=0)
    wait_bytes(ar_c.at[pl.ds(0, nl - 1)], arr_sem.at[2])
    for t in range(32):
        r, c = t // 2, t % 2
        piece = ar_c[t // per, 8 * (t % per) : 8 * (t % per) + 8, :]
        if r < 8:
            out_out[8 * r : 8 * r + 8, 128 * c : 128 * c + 128] = piece
        else:
            out_in[8 * r - 64 : 8 * r - 56, 128 * c : 128 * c + 128] = piece

    def sent(jp, carry):
        wait_bytes(sf.at[jp, pl.ds(0, ng - 1)], send1.at[jp])
        wait_bytes(sg.at[jp, pl.ds(0, ng - 1)], send2.at[jp])
        return carry

    lax.fori_loop(0, JP, sent, 0)
    wait_bytes(lrow1.at[pl.ds(0, nl - 1)], ls_sem.at[0])
    wait_bytes(lrow2.at[pl.ds(0, nm - 1)], ls_sem.at[1])
    wait_bytes(ar_a.at[pl.ds(0, nl - 1)], as_sem.at[0])
    wait_bytes(ar_b.at[pl.ds(0, nm - 1)], as_sem.at[1])
    wait_bytes(ar_c.at[pl.ds(0, nl - 1)], as_sem.at[2])


def body(nm, nl, state, target, w_in, w_out, legendre, wavenumber_of):
    _, channels, hemis, rows, nlon = state.shape
    slots, deg, nj = legendre.shape
    waves = slots * nl
    cols = 2 * waves
    ng = 2 * nl
    base = jnp.asarray(base_table(nlon, waves))
    order = wavenumber_of.reshape(nl, 2, 1, 4).transpose(1, 0, 2, 3)
    order = jnp.broadcast_to(order, (2, nl, 2, 4)).reshape(cols, 1)
    wcol = jnp.broadcast_to(order, (cols, 128))
    vmem = pl.BlockSpec(memory_space=pltpu.VMEM)
    hbm = pl.BlockSpec(memory_space=pl.ANY)
    dma = pltpu.SemaphoreType.DMA
    piece = 8 * (32 // nl)
    v = pltpu.VMEM
    grad_in, grad_out, loss = pl.pallas_call(
        functools.partial(kernel, nm, nl),
        out_shape=(
            jax.ShapeDtypeStruct((64, 256), F32),
            jax.ShapeDtypeStruct((64, 256), F32),
            jax.ShapeDtypeStruct((1, 128), F32),
        ),
        in_specs=[hbm, hbm, vmem, vmem, hbm, hbm, vmem],
        out_specs=(vmem, vmem, vmem),
        scratch_shapes=[
            v((channels, hemis, rows, nlon), BF16),
            v((nlon // 128, channels * hemis * rows, 128), F32),
            v((JP, 256, nlon), BF16),
            v((cols, nlon), BF16),
            v((cols, nlon), BF16),
            v((nlon, cols), BF16),
            v((256, 1024), BF16),
            v((1024, 256), BF16),
            v((256, 1024), BF16),
            v((JP, nlon, 1024), BF16),
            v((JP, nlon, 1024), BF16),
            v((nlon, 256), BF16),
            v((JP, ng, 16, 128), BF16),
            v((JP, ng, 16, 128), BF16),
            v((ng, 64, 128), F32),
            v((ng, 64, 128), F32),
            v((JP, ng, 16, 128), BF16),
            v((JP, ng, 16, 128), BF16),
            v((4, deg, nj), BF16),
            v((4, nj, deg), BF16),
            v((2, channels, slots, deg), BF16),
            v((deg // 128, 2 * channels * slots, 128), F32),
            v((8, deg, 256), BF16),
            v((4, 2, deg, 256), F32),
            v((4, 2, deg, 256), BF16),
            v((cols, 256), BF16),
            v((128, 256), F32),
            v((1, 128), F32),
            v((nl, 1, 128), F32),
            v((1, 128), F32),
            v((nm, 1, 128), F32),
            v((nl, piece, 128), F32),
            v((nl, piece, 128), F32),
            v((piece, 128), F32),
            v((nm, piece, 128), F32),
            v((piece, 128), F32),
            v((nl, piece, 128), F32),
            dma((4,)), dma((JP,)), dma((JP,)), dma((JP,)), dma((JP,)),
            dma((2,)), dma((2,)), dma((3,)), dma((3,)),
        ],
        compiler_params=pltpu.CompilerParams(
            collective_id=0, has_side_effects=True, vmem_limit_bytes=60 * 1024 * 1024
        ),
    )(state[0], target, w_in, w_out, legendre, base, wcol)
    groups = nm // 2
    scale = 0.5 / (groups * channels) / (waves * deg)
    return jnp.sum(loss) * scale, grad_in, grad_out.T


def solution(mesh):
    return jax.shard_map(
        functools.partial(body, mesh.shape["member"], mesh.shape["lat"]),
        mesh=mesh,
        in_specs=(
            P("member", None, None, "lat", None),
            P(None, None, "lat", None),
            P(),
            P(),
            P("lat", None, None),
            P(),
        ),
        out_specs=(P(), P(), P()),
        check_vma=False,
    )
```

```python
import functools
import math

import jax
import jax.numpy as jnp
import numpy as np
from jax import lax
from jax.experimental import pallas as pl
from jax.experimental.pallas import tpu as pltpu
from jax.sharding import PartitionSpec as P

MESH = pl.DeviceIdType.MESH
F32 = jnp.float32
BF16 = jnp.bfloat16
XC = 256


def dot(a, b):
    return jnp.dot(a, b, preferred_element_type=F32)


def base_table(nlon, waves):
    cell = np.arange(nlon, dtype=np.int64)[None, :]
    wave = np.arange(waves, dtype=np.int64)[:, None]
    angle = (cell * wave % nlon).astype(np.float32) * np.float32(2.0 * math.pi / nlon)
    both = np.concatenate([np.cos(angle), -np.sin(angle)], axis=0) / np.float32(math.sqrt(nlon))
    return both.astype(jnp.bfloat16)


def kernel(
    nm, nl, state_hbm, target_hbm, w_in_ref, w_out_ref, leg_hbm, base_hbm, wn_ref,
    out_in, out_out, out_loss,
    st_raw, st32, s_cx, base, wcol, wave_t, wave, w_in_bd, w_out_bd, w_pull, hid, slope, fore, gfull,
    hold, sf, rf, rf_a, rf_b, fg_a, fg_b, sg, rg, leg, leg_p, leg_t, tgt, tw, tgt_t, acc32, gb, bs,
    acc_out, acc_in, lsend, lrow1, lsend2, lrow2, ar_s, ar_a, ar_p, ar_b, ar_q, ar_c,
    in_sem, send1, recv1, send2, recv2, ls_sem, lr_sem, as_sem, ar_sem,
):
    member = lax.axis_index("member")
    lat = lax.axis_index("lat")
    half = lax.rem(member, 2)
    base_member = member - half
    ng = 2 * nl
    me = half * nl + lat
    nlon = wave.shape[0]
    cols = wave.shape[1]
    waves = cols // 2
    deg = leg.shape[1]
    nj = leg.shape[2]

    def at64(t):
        return (base_member + t // nl, lax.rem(t, nl))

    c_state = pltpu.make_async_copy(state_hbm, st_raw, in_sem.at[0])
    c_base = pltpu.make_async_copy(base_hbm, base, in_sem.at[1])
    c_leg = pltpu.make_async_copy(leg_hbm.at[pl.ds(half * 4, 4)], leg, in_sem.at[2])
    c_tgt = pltpu.make_async_copy(target_hbm, tgt, in_sem.at[3])
    c_state.start()
    c_base.start()
    c_leg.start()
    c_tgt.start()

    barrier = pltpu.get_barrier_semaphore()

    def greet(d, carry):
        pl.semaphore_signal(barrier, inc=1, device_id=at64(lax.rem(me + d, ng)), device_id_type=MESH)
        return carry

    lax.fori_loop(1, ng, greet, 0)

    def greet_member(d, carry):
        other = lax.rem(base_member + d, nm)
        pl.semaphore_signal(barrier, inc=1, device_id=(other, lat), device_id_type=MESH)
        return carry

    lax.fori_loop(2, nm, greet_member, 0)

    w_in_bd[...] = jnp.zeros_like(w_in_bd)
    w_pull[...] = jnp.zeros_like(w_pull)
    tall = w_out_ref[...].astype(F32)
    wide = jnp.concatenate([tall, tall, tall, tall], axis=0).T
    lane_group = lax.broadcasted_iota(jnp.int32, wide.shape, 1) >> 6
    for g in range(4):
        w_in_bd[64 * g : 64 * g + 64, 256 * g : 256 * g + 256] = w_in_ref[...]
        w_pull[64 * g : 64 * g + 64, 256 * g : 256 * g + 256] = w_out_ref[...]
        w_out_bd[256 * g : 256 * g + 256, :] = jnp.where(lane_group == g, wide, 0.0).astype(BF16)

    rows_of = [
        jnp.broadcast_to(wn_ref[r : r + 1, :].astype(F32), (128, 128)).T for r in range(wn_ref.shape[0])
    ]
    by_owner = jnp.concatenate(rows_of, axis=0).reshape(nl, 8, 128)
    sub = lax.broadcasted_iota(jnp.int32, (nl, 8, 128), 1)
    r2, r4, r6 = (pltpu.roll(by_owner, k, axis=1) for k in (2, 4, 6))
    first = jnp.where(sub < 2, by_owner, jnp.where(sub < 6, r2, r4))
    second = jnp.where(sub < 2, r4, jnp.where(sub < 6, r6, by_owner))
    wcol[: nl * 8] = first.reshape(nl * 8, 128)
    wcol[nl * 8 :] = second.reshape(nl * 8, 128)

    c_state.wait()

    def widen(xt, carry):
        lanes = pl.ds(pl.multiple_of(xt * 128, 128), 128)
        st32[xt] = st_raw[:, :, :, lanes].astype(F32).reshape(st32.shape[1], 128)
        return carry

    lax.fori_loop(0, nlon // 128, widen, 0)

    c_base.wait()
    lb = min(128, waves)
    rb = min(128, cols)

    def order_rows(r, carry):
        rows = pl.ds(pl.multiple_of(r * rb, rb), rb)
        number = wcol[rows, :][:, :lb]
        part = (lax.broadcasted_iota(jnp.int32, (rb, lb), 0) >> 1) & 1
        lane = lax.broadcasted_iota(jnp.int32, (rb, lb), 1)
        blocks = []
        for b in range(cols // lb):
            q, start = b * lb // waves, b * lb % waves
            same = number == (lane + start).astype(F32)
            blocks.append(jnp.where(same & (part == q), 1.0, 0.0))
        pick = jnp.concatenate(blocks, axis=1).astype(BF16)
        wave_t[rows, :] = dot(pick, base[...]).astype(BF16)
        return carry

    lax.fori_loop(0, cols // rb, order_rows, 0)

    spans = ((1, ng // 2), (ng // 2, ng))

    def send_half(tile, hf, src, dst, ssem, rsem):
        def one(d, carry):
            t = lax.rem(me + d, ng)
            pltpu.make_async_remote_copy(
                src_ref=src.at[tile, t], dst_ref=dst.at[tile, me],
                send_sem=ssem.at[2 * tile + hf], recv_sem=rsem.at[tile],
                device_id=at64(t), device_id_type=MESH,
            ).start()
            return carry

        lax.fori_loop(*spans[hf], one, 0)

    def send_tile(tile, src, dst, ssem, rsem):
        send_half(tile, 0, src, dst, ssem, rsem)
        send_half(tile, 1, src, dst, ssem, rsem)
        dst[tile, me] = src[tile, me]

    def wait_bytes(ref, sem):
        pltpu.make_async_copy(ref, ref, sem).wait()

    def left(tile, hf, src, ssem):
        wait_bytes(src.at[tile, pl.ds(0, spans[hf][1] - spans[hf][0])], ssem.at[2 * tile + hf])

    def here(tile, dst, rsem):
        wait_bytes(dst.at[tile, pl.ds(0, ng - 1)], rsem.at[tile])

    out1 = (sf, rf, send1, recv1)
    out2 = (sg, rg, send2, recv2)
    low4 = lax.broadcasted_iota(jnp.int32, (ng, 8, 128), 1) < 4

    def forward(jp, carry):
        def network(xc, inner):
            rows = pl.ds(pl.multiple_of(xc * XC, XC), XC)
            turned = []
            for xt in range(XC // 128):
                tile = xc * (XC // 128) + xt
                parts = [
                    st32[tile, pl.ds(h * 8 + jp * 2 + j2, 64, stride=16), :]
                    for j2 in range(2) for h in range(2)
                ]
                block = jnp.concatenate(parts, axis=0)
                s_cx[jp, :, pl.ds(pl.multiple_of(tile * 128, 128), 128)] = block.astype(BF16)
                turned.append(block.T)
            field = jnp.concatenate(turned, axis=0)
            pre = dot(field.astype(BF16), w_in_bd[...])
            sig = 0.5 + 0.5 * jnp.tanh(0.5 * pre)
            hidden = (pre * sig).astype(BF16)
            hid[jp, rows, :] = hidden
            slope[jp, rows, :] = (sig * (1.0 + pre * (1.0 - sig))).astype(BF16)
            fore[rows, :] = (field + dot(hidden, w_out_bd[...])).astype(BF16)
            return inner

        lax.fori_loop(0, nlon // XC, network, 0)
        modes = dot(wave_t[...], fore[...])
        one, two = modes[:, :128].reshape(ng, 8, 128), modes[:, 128:].reshape(ng, 8, 128)

        @pl.when(jp == 0)
        def _():
            pl.semaphore_wait(barrier, ng - 1 + nm - 2)

        @pl.when(jp < 2)
        def _():
            sf[jp] = jnp.concatenate([one, two], axis=1).astype(BF16)
            send_tile(jp, *out1)

        @pl.when(jp >= 2)
        def _():
            hold[jp - 2, 0] = jnp.where(low4, one, pltpu.roll(two, 4, axis=1))
            hold[jp - 2, 1] = jnp.where(low4, pltpu.roll(one, 4, axis=1), two)

        return carry

    lax.fori_loop(0, 4, forward, 0)
    for ig in range(2):
        sf[2 + ig] = jnp.concatenate([hold[0, ig], hold[1, ig]], axis=1).astype(BF16)
    send_tile(2, *out1)

    c_leg.wait()
    c_tgt.wait()
    col = lax.broadcasted_iota(jnp.int32, (nj, nj), 1)
    row = lax.broadcasted_iota(jnp.int32, (nj, nj), 0)
    from_col = jnp.where(col >= 4 * nl, col - 4 * nl, col)
    wanted = (from_col >> 2) * 8 + (from_col & 3) + jnp.where(col >= 4 * nl, 4, 0)
    perm = jnp.where(row == wanted, 1.0, 0.0).astype(BF16)
    for i in range(4):
        moved = dot(leg[i], perm)
        leg_p[i] = moved.astype(BF16)
        leg_t[i] = moved.T.astype(BF16)
    for b in range(deg // 128):
        tw[b] = tgt[:, :, :, 128 * b : 128 * b + 128].astype(F32).reshape(tw.shape[1], 128)
    for b in range(deg // 128):
        for i in range(8):
            parts = [tw[b, pl.ds(q * 512 + i, 64, stride=8), :] for q in (0, 0, 1, 1)]
            tgt_t[i, 128 * b : 128 * b + 128, :] = jnp.concatenate(parts, axis=0).T.astype(BF16)

    left(1, 0, sf, send1)
    left(1, 1, sf, send1)
    send_half(3, 0, *out1)
    rf[3, me] = sf[3, me]

    def turn_wave(xt, carry):
        start = pl.multiple_of(xt * 128, 128)
        wave[pl.ds(start, 128), :] = wave_t[:, pl.ds(start, 128)].astype(F32).T.astype(BF16)
        return carry

    lax.fori_loop(0, nlon // 128, turn_wave, 0)
    acc_out[...] = jnp.zeros_like(acc_out)
    acc_in[...] = jnp.zeros_like(acc_in)
    left(2, 0, sf, send1)
    send_half(3, 1, *out1)

    for t in range(2):
        here(t, rf, recv1)
        rf_a[:, 16 * t : 16 * t + 16, :] = rf[t].astype(F32)

    own = wcol[pl.ds(pl.multiple_of(me * 8, 8), 8), :].astype(jnp.int32)
    obj = 1.0 / ((nm // 2) * 64)
    nb = 64
    flat_a = rf_a.reshape(ng * 32, 128)
    flat_ga = fg_a.reshape(ng * 32, 128)

    def middle(ig, loss8):
        here(2 + ig, rf, recv1)
        rf_b[ig] = rf[2 + ig].astype(F32)
        flat_b = rf_b.at[ig].reshape(ng * 16, 128)
        flat_gb = fg_b.at[ig].reshape(ng * 16, 128)
        for i2 in range(2):
            for e in range(2):
                early = [
                    flat_a[pl.ds(e * nl * 32 + ig * 4 + q * 2 + i2, nl * 4, stride=8), :] for q in range(2)
                ]
                late = [flat_b[pl.ds(e * nl * 16 + q * 2 + i2, nl * 4, stride=4), :] for q in range(2)]
                modes = jnp.concatenate(
                    [jnp.concatenate(early, axis=1), jnp.concatenate(late, axis=1)], axis=0
                )
                acc32[i2, e] = dot(leg_p[2 * ig + i2], modes.astype(BF16))

        def compare(c, carry):
            rows = pl.ds(pl.multiple_of(c * nb, nb), nb)
            degree = lax.broadcasted_iota(jnp.int32, (nb, 128), 0) + c * nb
            south = lax.broadcasted_iota(jnp.int32, (nb, 128), 1) >= 64
            loss = jnp.zeros((nb, 128), F32)
            for i2 in range(2):
                gap = degree - own[4 * ig + i2 : 4 * ig + i2 + 1, :]
                live = gap >= 0
                sign = jnp.where((gap & 1) == 0, 1.0, -1.0)
                turn = jnp.where(south, sign, 1.0)
                for q in range(2):
                    lanes = slice(128 * q, 128 * q + 128)
                    coeffs = []
                    for e in range(2):
                        part = acc32[i2, e, rows, lanes]
                        whole = part + sign * pltpu.roll(part, 64, axis=1)
                        coeffs.append(jnp.where(live, whole, 0.0).astype(BF16).astype(F32))
                    aim = tgt_t[half * 4 + 2 * ig + i2, rows, lanes].astype(F32) * turn
                    d0, d1, ds = coeffs[0] - aim, coeffs[1] - aim, coeffs[0] - coeffs[1]
                    u0, u1, us = d0 * d0 + 1.0, d1 * d1 + 1.0, ds * ds + 1.0
                    r0, r1, rs = lax.rsqrt(u0), lax.rsqrt(u1), lax.rsqrt(us)
                    term = 0.5 * ((u0 * r0 - 1.0) + (u1 * r1 - 1.0) - (us * rs - 1.0))
                    loss = loss + jnp.where(live, term, 0.0)
                    pull = 0.5 * (ds * rs)
                    gb[i2, 0, rows, lanes] = jnp.where(live, (0.5 * (d0 * r0) - pull) * obj, 0.0).astype(BF16)
                    gb[i2, 1, rows, lanes] = jnp.where(live, (0.5 * (d1 * r1) + pull) * obj, 0.0).astype(BF16)
            return carry + jnp.sum(loss.reshape(nb // 8, 8, 128), axis=0)

        loss8 = lax.fori_loop(0, deg // nb, compare, loss8)
        for i2 in range(2):
            for e in range(2):
                back = dot(leg_t[2 * ig + i2], gb[i2, e])
                for q in range(2):
                    lanes = slice(128 * q, 128 * q + 128)
                    flat_gb[pl.ds(e * nl * 16 + q * 2 + i2, nl * 4, stride=4), :] = back[: nl * 4, lanes]
                    flat_ga[pl.ds(e * nl * 32 + ig * 4 + q * 2 + i2, nl * 4, stride=8), :] = back[nl * 4 :, lanes]
        sg[ig] = fg_b[ig].astype(BF16)
        send_tile(ig, *out2)
        return loss8

    loss8 = middle(0, jnp.zeros((8, 128), F32))
    loss8 = middle(1, loss8)
    for t in range(2):
        sg[2 + t] = fg_a[:, 16 * t : 16 * t + 16, :].astype(BF16)
        rg[2 + t, me] = sg[2 + t, me]

    def to_lats(src_of, dst, ssem, rsem):
        def one(d, carry):
            t = lax.rem(lat + d, nl)
            pltpu.make_async_remote_copy(
                src_ref=src_of(t), dst_ref=dst.at[lat], send_sem=ssem, recv_sem=rsem,
                device_id=(member, t), device_id_type=MESH,
            ).start()
            return carry

        lax.fori_loop(1, nl, one, 0)

    def to_members(src, dst, ssem, rsem):
        def one(d, carry):
            t = lax.rem(member + d, nm)
            pltpu.make_async_remote_copy(
                src_ref=src, dst_ref=dst.at[member], send_sem=ssem, recv_sem=rsem,
                device_id=(t, lat), device_id_type=MESH,
            ).start()
            return carry

        lax.fori_loop(1, nm, one, 0)

    lsend[...] = jnp.sum(loss8, axis=0, keepdims=True)
    to_lats(lambda t: lsend, lrow1, ls_sem.at[0], lr_sem.at[0])
    lrow1[lat] = lsend[...]

    left(0, 0, sg, send2)
    left(0, 1, sg, send2)
    send_half(2, 0, *out2)
    left(1, 0, sg, send2)
    send_half(2, 1, *out2)

    per = 8 // ar_s.shape[2]
    step = ar_s.shape[2]

    def share(k, acc):
        for t in range(16):
            r, c = t // 2, t % 2
            for u in range(per):
                ar_s[k, t * per + u] = acc[8 * r + step * u : 8 * r + step * u + step, 128 * c : 128 * c + 128]
        to_lats(lambda t: ar_s.at[k, t], ar_a.at[k], as_sem.at[3 * k], ar_sem.at[3 * k])
        ar_a[k, lat] = ar_s[k, lat]

    def backward(jp, last=False):
        if jp < 2:
            even = jp * 8
            va = rg[0].astype(F32)[:, even : even + 8]
            vb = rg[1].astype(F32)[:, even : even + 8]
            one = jnp.where(low4, va, pltpu.roll(vb, 4, axis=1))
            two = jnp.where(low4, pltpu.roll(va, 4, axis=1), vb)
        else:
            block = rg[jp].astype(F32)
            one, two = block[:, :8], block[:, 8:]
        bs[:, :128] = one.reshape(cols, 128).astype(BF16)
        bs[:, 128:] = two.reshape(cols, 128).astype(BF16)

        def out_step(xc, inner):
            rows = pl.ds(pl.multiple_of(xc * XC, XC), XC)
            grad = dot(wave[rows, :], bs[...])
            grad16 = grad.astype(BF16)
            gfull[rows, :] = grad16
            turned = grad16.astype(F32).T.astype(BF16)
            total = jnp.zeros((64, 256), F32)
            for g in range(4):
                total = total + dot(turned[64 * g : 64 * g + 64], hid[jp, rows, 256 * g : 256 * g + 256])
            acc_out[...] += total
            return inner

        def in_step(xc, inner):
            rows = pl.ds(pl.multiple_of(xc * XC, XC), XC)
            act = (dot(gfull[rows, :], w_pull[...]) * slope[jp, rows, :].astype(F32)).astype(BF16)
            total = jnp.zeros((64, 256), F32)
            for g in range(4):
                total = total + dot(s_cx[jp, 64 * g : 64 * g + 64, rows], act[:, 256 * g : 256 * g + 256])
            acc_in[...] += total
            return inner

        lax.fori_loop(0, nlon // XC, out_step, 0)
        if last:
            share(0, acc_out)
        lax.fori_loop(0, nlon // XC, in_step, 0)

    here(0, rg, recv2)
    here(1, rg, recv2)
    left(1, 1, sg, send2)
    send_half(3, 0, *out2)
    backward(0)
    left(2, 0, sg, send2)
    send_half(3, 1, *out2)
    backward(1)
    wait_bytes(lrow1.at[pl.ds(0, nl - 1)], lr_sem.at[0])
    lsend2[...] = jnp.sum(lrow1[...], axis=0)
    to_members(lsend2, lrow2, ls_sem.at[1], lr_sem.at[1])
    lrow2[member] = lsend2[...]
    here(2, rg, recv2)
    backward(2)
    here(3, rg, recv2)
    backward(3, True)

    share(1, acc_in)
    for k in range(2):
        wait_bytes(ar_a.at[k, pl.ds(0, nl - 1)], ar_sem.at[3 * k])
        ar_p[k] = jnp.sum(ar_a[k], axis=0)
        to_members(ar_p.at[k], ar_b.at[k], as_sem.at[3 * k + 1], ar_sem.at[3 * k + 1])
        ar_b[k, member] = ar_p[k]
    for k in range(2):
        wait_bytes(ar_b.at[k, pl.ds(0, nm - 1)], ar_sem.at[3 * k + 1])
        ar_q[k] = jnp.sum(ar_b[k], axis=0)
        to_lats(lambda t: ar_q.at[k], ar_c.at[k], as_sem.at[3 * k + 2], ar_sem.at[3 * k + 2])
        ar_c[k, lat] = ar_q[k]
    wait_bytes(lrow2.at[pl.ds(0, nm - 1)], lr_sem.at[1])
    out_loss[...] = jnp.sum(lrow2[...], axis=0)
    for t in range(4):
        for hf in range(2):
            if (t, hf) not in ((1, 0), (1, 1), (2, 0)):
                left(t, hf, sf, send1)
            if (t, hf) not in ((0, 0), (0, 1), (1, 0), (1, 1), (2, 0)):
                left(t, hf, sg, send2)
    wait_bytes(lrow1.at[pl.ds(0, nl - 1)], ls_sem.at[0])
    wait_bytes(lrow2.at[pl.ds(0, nm - 1)], ls_sem.at[1])
    for k, out in ((0, out_out), (1, out_in)):
        wait_bytes(ar_c.at[k, pl.ds(0, nl - 1)], ar_sem.at[3 * k + 2])
        for t in range(16):
            r, c = t // 2, t % 2
            for u in range(per):
                out[8 * r + step * u : 8 * r + step * u + step, 128 * c : 128 * c + 128] = ar_c[k, t * per + u]
    for k in range(2):
        wait_bytes(ar_a.at[k, pl.ds(0, nl - 1)], as_sem.at[3 * k])
        wait_bytes(ar_b.at[k, pl.ds(0, nm - 1)], as_sem.at[3 * k + 1])
        wait_bytes(ar_c.at[k, pl.ds(0, nl - 1)], as_sem.at[3 * k + 2])


def finish(scale, g_in, g_out, loss, o_in, o_out, o_loss):
    o_in[...] = g_in[...]
    o_out[...] = g_out[...]
    o_loss[...] = jnp.sum(loss[...], axis=1, keepdims=True) * scale


def body(nm, nl, state, target, w_in, w_out, legendre, wavenumber_of):
    _, channels, hemis, rows, nlon = state.shape
    slots, deg, nj = legendre.shape
    waves = slots * nl
    cols = 2 * waves
    ng = 2 * nl
    base = jnp.asarray(base_table(nlon, waves))
    vmem = pl.BlockSpec(memory_space=pltpu.VMEM)
    hbm = pl.BlockSpec(memory_space=pl.ANY)
    dma = pltpu.SemaphoreType.DMA
    piece = 128 // nl
    v = pltpu.VMEM
    sums = (
        jax.ShapeDtypeStruct((64, 256), F32),
        jax.ShapeDtypeStruct((64, 256), F32),
        jax.ShapeDtypeStruct((1, 128), F32),
    )
    parts = pl.pallas_call(
        functools.partial(kernel, nm, nl),
        out_shape=sums,
        in_specs=[hbm, hbm, vmem, vmem, hbm, hbm, vmem],
        out_specs=(vmem, vmem, vmem),
        scratch_shapes=[
            v((channels, hemis, rows, nlon), BF16),
            v((nlon // 128, channels * hemis * rows, 128), F32),
            v((4, 256, nlon), BF16),
            v((cols, nlon), BF16),
            v((cols, 128), F32),
            v((cols, nlon), BF16),
            v((nlon, cols), BF16),
            v((256, 1024), BF16),
            v((1024, 256), BF16),
            v((256, 1024), BF16),
            v((4, nlon, 1024), BF16),
            v((4, nlon, 1024), BF16),
            v((nlon, 256), BF16),
            v((nlon, 256), BF16),
            v((2, 2, ng, 8, 128), F32),
            v((4, ng, 16, 128), BF16),
            v((4, ng, 16, 128), BF16),
            v((ng, 32, 128), F32),
            v((2, ng, 16, 128), F32),
            v((ng, 32, 128), F32),
            v((2, ng, 16, 128), F32),
            v((4, ng, 16, 128), BF16),
            v((4, ng, 16, 128), BF16),
            v((4, deg, nj), BF16),
            v((4, deg, nj), BF16),
            v((4, nj, deg), BF16),
            v((2, channels, slots, deg), BF16),
            v((deg // 128, 2 * channels * slots, 128), F32),
            v((8, deg, 256), BF16),
            v((2, 2, deg, 256), F32),
            v((2, 2, deg, 256), BF16),
            v((cols, 256), BF16),
            v((64, 256), F32),
            v((64, 256), F32),
            v((1, 128), F32),
            v((nl, 1, 128), F32),
            v((1, 128), F32),
            v((nm, 1, 128), F32),
            v((2, nl, piece, 128), F32),
            v((2, nl, piece, 128), F32),
            v((2, piece, 128), F32),
            v((2, nm, piece, 128), F32),
            v((2, piece, 128), F32),
            v((2, nl, piece, 128), F32),
            dma((4,)), dma((8,)), dma((4,)), dma((8,)), dma((4,)),
            dma((2,)), dma((2,)), dma((6,)), dma((6,)),
        ],
        compiler_params=pltpu.CompilerParams(
            collective_id=0, has_side_effects=True, vmem_limit_bytes=60 * 1024 * 1024
        ),
    )(state[0], target, w_in, w_out.T, legendre, base, wavenumber_of.reshape(-1, 128))
    scale = 0.5 / ((nm // 2) * channels) / (waves * deg)
    grad_in, grad_out, loss = pl.pallas_call(
        functools.partial(finish, scale),
        out_shape=(sums[0], sums[1], jax.ShapeDtypeStruct((1, 1), F32)),
        in_specs=[vmem, vmem, vmem],
        out_specs=(vmem, vmem, vmem),
    )(*parts)
    return loss.reshape(()), grad_in, grad_out.T


def solution(mesh):
    return jax.shard_map(
        functools.partial(body, mesh.shape["member"], mesh.shape["lat"]),
        mesh=mesh,
        in_specs=(
            P("member", None, None, "lat", None),
            P(None, None, "lat", None),
            P(),
            P(),
            P("lat", None, None),
            P(),
        ),
        out_specs=(P(), P(), P()),
        check_vma=False,
    )
```

```python
import functools
import math

import jax
import jax.numpy as jnp
import numpy as np
from jax import lax
from jax.experimental import pallas as pl
from jax.experimental.pallas import tpu as pltpu
from jax.sharding import PartitionSpec as P

MESH = pl.DeviceIdType.MESH
F32 = jnp.float32
BF16 = jnp.bfloat16
XC = 1024


def dot(a, b):
    return jnp.dot(a, b, preferred_element_type=F32)


def base_table(nlon, waves):
    cell = np.arange(nlon, dtype=np.int64)[None, :]
    wave = np.arange(waves, dtype=np.int64)[:, None]
    angle = (cell * wave % nlon).astype(np.float32) * np.float32(2.0 * math.pi / nlon)
    both = np.concatenate([np.cos(angle), -np.sin(angle)], axis=0) / np.float32(math.sqrt(nlon))
    return both.astype(jnp.bfloat16)


def kernel(
    nm, nl, state_hbm, target_hbm, w_in_ref, w_out_ref, leg_hbm, base_hbm, wn_ref,
    out_in, out_out, out_loss,
    st_raw, st32, s_cx, base, wcol, wave_t, wave, w_in_bd, w_out_bd, w_pull, hid, slope, fore, gfull,
    hold, sf, rf, rf_a, rf_b, fg_a, fg_b, sg, rg, leg, leg_p, leg_t, tgt, tw, tgt_t, acc32, gb, bs,
    acc_out, acc_in, lsend, lrow1, lsend2, lrow2, ar_s, ar_a, ar_p, ar_b, ar_q, ar_c,
    in_sem, send1, recv1, send2, recv2, ls_sem, lr_sem, as_sem, ar_sem,
):
    member = lax.axis_index("member")
    lat = lax.axis_index("lat")
    half = lax.rem(member, 2)
    base_member = member - half
    ng = 2 * nl
    me = half * nl + lat
    nlon = wave.shape[0]
    cols = wave.shape[1]
    waves = cols // 2
    deg = leg.shape[1]
    nj = leg.shape[2]

    ny, nz = nl // 4, nm // 2
    my_core, my_y, my_x, my_z = lax.rem(lat, 2), lax.rem(lat // 2, ny), lat // (2 * ny), member // 2
    members = (member, base_member + 1 - half)
    halves = (half, 1 - half)
    beside = [[x * 2 * ny + c for c in (my_core, 1 - my_core)] for x in (my_x, 1 - my_x)]

    def ring(i, size):
        return size // 2 + (1 - 2 * lax.rem(i, 2)) * ((i + 1) // 2)

    def wrap(v, size):
        return jnp.where(v >= size, v - size, v)

    def around(size, lo, hi, act):
        if hi > lo:
            lax.fori_loop(lo, min(hi, size - 1), lambda i, carry: (act(i, False), carry)[1], 0)
        if hi == size:
            act(size - 1, True)

    def group_step(act):
        def at(i, stay):
            y = wrap(my_y + ring(i, ny), ny) * 2
            for h in range(2):
                for x in range(2):
                    for c in range(2):
                        if not (stay and h == x == c == 0):
                            there = beside[x][c] + y
                            act((members[h], there), halves[h] * nl + there)

        return at

    def lat_step(act):
        def at(i, stay):
            y = wrap(my_y + ring(i, ny), ny) * 2
            for x in range(2):
                for c in range(2):
                    if not (stay and x == c == 0):
                        act(beside[x][c] + y)

        return at

    def member_step(act):
        def at(i, stay):
            z = wrap(my_z + ring(i, nz), nz) * 2
            for h in range(2):
                if not (stay and h == 0):
                    act(z + halves[h])

        return at

    c_state = pltpu.make_async_copy(state_hbm, st_raw, in_sem.at[0])
    c_base = pltpu.make_async_copy(base_hbm, base, in_sem.at[1])
    c_leg = pltpu.make_async_copy(leg_hbm.at[pl.ds(half * 4, 4)], leg, in_sem.at[2])
    c_tgt = pltpu.make_async_copy(target_hbm, tgt, in_sem.at[3])
    c_state.start()
    c_base.start()
    c_leg.start()
    c_tgt.start()

    barrier = pltpu.get_barrier_semaphore()

    def greet(there):
        pl.semaphore_signal(barrier, inc=1, device_id=there, device_id_type=MESH)

    around(ny, 0, ny, group_step(lambda there, t: greet(there)))
    for d in range(1, nz):
        for h in range(2):
            greet((wrap(my_z + d, nz) * 2 + h, lat))

    w_in_bd[...] = jnp.zeros_like(w_in_bd)
    w_pull[...] = jnp.zeros_like(w_pull)
    tall = w_out_ref[...].astype(F32)
    wide = jnp.concatenate([tall, tall, tall, tall], axis=0).T
    lane_group = lax.broadcasted_iota(jnp.int32, wide.shape, 1) >> 6
    for g in range(4):
        w_in_bd[64 * g : 64 * g + 64, 256 * g : 256 * g + 256] = w_in_ref[...]
        w_pull[64 * g : 64 * g + 64, 256 * g : 256 * g + 256] = w_out_ref[...]
        w_out_bd[256 * g : 256 * g + 256, :] = jnp.where(lane_group == g, wide, 0.0).astype(BF16)

    rows_of = [
        jnp.broadcast_to(wn_ref[r : r + 1, :].astype(F32), (128, 128)).T for r in range(wn_ref.shape[0])
    ]
    by_owner = jnp.concatenate(rows_of, axis=0).reshape(nl, 8, 128)
    sub = lax.broadcasted_iota(jnp.int32, (nl, 8, 128), 1)
    r2, r4, r6 = (pltpu.roll(by_owner, k, axis=1) for k in (2, 4, 6))
    first = jnp.where(sub < 2, by_owner, jnp.where(sub < 6, r2, r4))
    second = jnp.where(sub < 2, r4, jnp.where(sub < 6, r6, by_owner))
    wcol[: nl * 8] = first.reshape(nl * 8, 128)
    wcol[nl * 8 :] = second.reshape(nl * 8, 128)

    c_state.wait()

    def widen(xt, carry):
        lanes = pl.ds(pl.multiple_of(xt * 128, 128), 128)
        st32[xt] = st_raw[:, :, :, lanes].astype(F32).reshape(st32.shape[1], 128)
        return carry

    lax.fori_loop(0, nlon // 128, widen, 0)

    c_base.wait()
    lb = min(128, waves)
    rb = min(128, cols)

    def order_rows(r, carry):
        rows = pl.ds(pl.multiple_of(r * rb, rb), rb)
        number = wcol[rows, :][:, :lb]
        part = (lax.broadcasted_iota(jnp.int32, (rb, lb), 0) >> 1) & 1
        lane = lax.broadcasted_iota(jnp.int32, (rb, lb), 1)
        blocks = []
        for b in range(cols // lb):
            q, start = b * lb // waves, b * lb % waves
            same = number == (lane + start).astype(F32)
            blocks.append(jnp.where(same & (part == q), 1.0, 0.0))
        pick = jnp.concatenate(blocks, axis=1).astype(BF16)
        wave_t[rows, :] = dot(pick, base[...]).astype(BF16)
        return carry

    lax.fori_loop(0, cols // rb, order_rows, 0)

    spans = ((0, ny // 2), (ny // 2, ny))
    counts = (ng // 2, ng // 2 - 1)

    def send_half(tile, hf, src, dst, ssem, rsem):
        def one(there, t):
            pltpu.make_async_remote_copy(
                src_ref=src.at[tile, t], dst_ref=dst.at[tile, me],
                send_sem=ssem.at[2 * tile + hf], recv_sem=rsem.at[tile],
                device_id=there, device_id_type=MESH,
            ).start()

        around(ny, *spans[hf], group_step(one))

    def send_tile(tile, src, dst, ssem, rsem):
        send_half(tile, 0, src, dst, ssem, rsem)
        send_half(tile, 1, src, dst, ssem, rsem)
        dst[tile, me] = src[tile, me]

    def wait_bytes(ref, sem):
        pltpu.make_async_copy(ref, ref, sem).wait()

    def left(tile, hf, src, ssem):
        wait_bytes(src.at[tile, pl.ds(0, counts[hf])], ssem.at[2 * tile + hf])

    def here(tile, dst, rsem):
        wait_bytes(dst.at[tile, pl.ds(0, ng - 1)], rsem.at[tile])

    out1 = (sf, rf, send1, recv1)
    out2 = (sg, rg, send2, recv2)
    low4 = lax.broadcasted_iota(jnp.int32, (ng, 8, 128), 1) < 4

    def forward(jp, carry):
        def network(xc, inner):
            rows = pl.ds(pl.multiple_of(xc * XC, XC), XC)
            turned = []
            for xt in range(XC // 128):
                tile = xc * (XC // 128) + xt
                parts = [
                    st32[tile, pl.ds(h * 8 + jp * 2 + j2, 64, stride=16), :]
                    for j2 in range(2) for h in range(2)
                ]
                block = jnp.concatenate(parts, axis=0)
                s_cx[jp, :, pl.ds(pl.multiple_of(tile * 128, 128), 128)] = block.astype(BF16)
                turned.append(block.T)
            field = jnp.concatenate(turned, axis=0)
            pre = dot(field.astype(BF16), w_in_bd[...])
            sig = 0.5 + 0.5 * jnp.tanh(0.5 * pre)
            hidden = (pre * sig).astype(BF16)
            hid[jp, rows, :] = hidden
            slope[jp, rows, :] = (sig * (1.0 + pre * (1.0 - sig))).astype(BF16)
            fore[rows, :] = (field + dot(hidden, w_out_bd[...])).astype(BF16)
            return inner

        lax.fori_loop(0, nlon // XC, network, 0)
        modes = dot(wave_t[...], fore[...])
        one, two = modes[:, :128].reshape(ng, 8, 128), modes[:, 128:].reshape(ng, 8, 128)

        @pl.when(jp == 0)
        def _():
            pl.semaphore_wait(barrier, ng - 1 + nm - 2)

        @pl.when(jp < 2)
        def _():
            sf[jp] = jnp.concatenate([one, two], axis=1).astype(BF16)
            send_tile(jp, *out1)

        @pl.when(jp >= 2)
        def _():
            hold[jp - 2, 0] = jnp.where(low4, one, pltpu.roll(two, 4, axis=1))
            hold[jp - 2, 1] = jnp.where(low4, pltpu.roll(one, 4, axis=1), two)

        return carry

    lax.fori_loop(0, 4, forward, 0)
    for ig in range(2):
        sf[2 + ig] = jnp.concatenate([hold[0, ig], hold[1, ig]], axis=1).astype(BF16)
    send_tile(2, *out1)

    c_leg.wait()
    c_tgt.wait()
    col = lax.broadcasted_iota(jnp.int32, (nj, nj), 1)
    row = lax.broadcasted_iota(jnp.int32, (nj, nj), 0)
    from_col = jnp.where(col >= 4 * nl, col - 4 * nl, col)
    wanted = (from_col >> 2) * 8 + (from_col & 3) + jnp.where(col >= 4 * nl, 4, 0)
    perm = jnp.where(row == wanted, 1.0, 0.0).astype(BF16)
    for i in range(4):
        moved = dot(leg[i], perm)
        leg_p[i] = moved.astype(BF16)
        leg_t[i] = moved.T.astype(BF16)
    for b in range(deg // 128):
        tw[b] = tgt[:, :, :, 128 * b : 128 * b + 128].astype(F32).reshape(tw.shape[1], 128)
    for b in range(deg // 128):
        for i in range(8):
            parts = [tw[b, pl.ds(q * 512 + i, 64, stride=8), :] for q in (0, 0, 1, 1)]
            tgt_t[i, 128 * b : 128 * b + 128, :] = jnp.concatenate(parts, axis=0).T.astype(BF16)

    left(1, 0, sf, send1)
    left(1, 1, sf, send1)
    send_half(3, 0, *out1)
    rf[3, me] = sf[3, me]

    def turn_wave(xt, carry):
        start = pl.multiple_of(xt * 128, 128)
        wave[pl.ds(start, 128), :] = wave_t[:, pl.ds(start, 128)].astype(F32).T.astype(BF16)
        return carry

    lax.fori_loop(0, nlon // 128, turn_wave, 0)
    acc_out[...] = jnp.zeros_like(acc_out)
    acc_in[...] = jnp.zeros_like(acc_in)
    left(2, 0, sf, send1)
    send_half(3, 1, *out1)

    for t in range(2):
        here(t, rf, recv1)
        rf_a[:, 16 * t : 16 * t + 16, :] = rf[t].astype(F32)

    own = wcol[pl.ds(pl.multiple_of(me * 8, 8), 8), :].astype(jnp.int32)
    obj = 1.0 / ((nm // 2) * 64)
    nb = 64
    flat_a = rf_a.reshape(ng * 32, 128)
    flat_ga = fg_a.reshape(ng * 32, 128)

    def middle(ig, loss8):
        here(2 + ig, rf, recv1)
        rf_b[ig] = rf[2 + ig].astype(F32)
        flat_b = rf_b.at[ig].reshape(ng * 16, 128)
        flat_gb = fg_b.at[ig].reshape(ng * 16, 128)
        for i2 in range(2):
            for e in range(2):
                early = [
                    flat_a[pl.ds(e * nl * 32 + ig * 4 + q * 2 + i2, nl * 4, stride=8), :] for q in range(2)
                ]
                late = [flat_b[pl.ds(e * nl * 16 + q * 2 + i2, nl * 4, stride=4), :] for q in range(2)]
                modes = jnp.concatenate(
                    [jnp.concatenate(early, axis=1), jnp.concatenate(late, axis=1)], axis=0
                )
                acc32[i2, e] = dot(leg_p[2 * ig + i2], modes.astype(BF16))

        def compare(c, carry):
            rows = pl.ds(pl.multiple_of(c * nb, nb), nb)
            degree = lax.broadcasted_iota(jnp.int32, (nb, 128), 0) + c * nb
            south = lax.broadcasted_iota(jnp.int32, (nb, 128), 1) >= 64
            loss = jnp.zeros((nb, 128), F32)
            for i2 in range(2):
                gap = degree - own[4 * ig + i2 : 4 * ig + i2 + 1, :]
                live = gap >= 0
                sign = jnp.where((gap & 1) == 0, 1.0, -1.0)
                turn = jnp.where(south, sign, 1.0)
                for q in range(2):
                    lanes = slice(128 * q, 128 * q + 128)
                    coeffs = []
                    for e in range(2):
                        part = acc32[i2, e, rows, lanes]
                        whole = part + sign * pltpu.roll(part, 64, axis=1)
                        coeffs.append(jnp.where(live, whole, 0.0).astype(BF16).astype(F32))
                    aim = tgt_t[half * 4 + 2 * ig + i2, rows, lanes].astype(F32) * turn
                    d0, d1, ds = coeffs[0] - aim, coeffs[1] - aim, coeffs[0] - coeffs[1]
                    u0, u1, us = d0 * d0 + 1.0, d1 * d1 + 1.0, ds * ds + 1.0
                    r0, r1, rs = lax.rsqrt(u0), lax.rsqrt(u1), lax.rsqrt(us)
                    term = 0.5 * ((u0 * r0 - 1.0) + (u1 * r1 - 1.0) - (us * rs - 1.0))
                    loss = loss + jnp.where(live, term, 0.0)
                    pull = 0.5 * (ds * rs)
                    gb[i2, 0, rows, lanes] = jnp.where(live, (0.5 * (d0 * r0) - pull) * obj, 0.0).astype(BF16)
                    gb[i2, 1, rows, lanes] = jnp.where(live, (0.5 * (d1 * r1) + pull) * obj, 0.0).astype(BF16)
            return carry + jnp.sum(loss.reshape(nb // 8, 8, 128), axis=0)

        loss8 = lax.fori_loop(0, deg // nb, compare, loss8)
        for i2 in range(2):
            for e in range(2):
                back = dot(leg_t[2 * ig + i2], gb[i2, e])
                for q in range(2):
                    lanes = slice(128 * q, 128 * q + 128)
                    flat_gb[pl.ds(e * nl * 16 + q * 2 + i2, nl * 4, stride=4), :] = back[: nl * 4, lanes]
                    flat_ga[pl.ds(e * nl * 32 + ig * 4 + q * 2 + i2, nl * 4, stride=8), :] = back[nl * 4 :, lanes]
        sg[ig] = fg_b[ig].astype(BF16)
        send_tile(ig, *out2)
        return loss8

    loss8 = middle(0, jnp.zeros((8, 128), F32))
    loss8 = middle(1, loss8)
    for t in range(2):
        sg[2 + t] = fg_a[:, 16 * t : 16 * t + 16, :].astype(BF16)
        rg[2 + t, me] = sg[2 + t, me]

    def to_lats(src_of, dst, ssem, rsem):
        def one(t):
            pltpu.make_async_remote_copy(
                src_ref=src_of(t), dst_ref=dst.at[lat], send_sem=ssem, recv_sem=rsem,
                device_id=(member, t), device_id_type=MESH,
            ).start()

        around(ny, 0, ny, lat_step(one))

    def to_members(src, dst, ssem, rsem):
        def one(t):
            pltpu.make_async_remote_copy(
                src_ref=src, dst_ref=dst.at[member], send_sem=ssem, recv_sem=rsem,
                device_id=(t, lat), device_id_type=MESH,
            ).start()

        around(nz, 0, nz, member_step(one))

    lsend[...] = jnp.sum(loss8, axis=0, keepdims=True)
    to_lats(lambda t: lsend, lrow1, ls_sem.at[0], lr_sem.at[0])
    lrow1[lat] = lsend[...]

    left(0, 0, sg, send2)
    left(0, 1, sg, send2)
    send_half(2, 0, *out2)
    left(1, 0, sg, send2)
    send_half(2, 1, *out2)

    chips = nl // 2
    tiles = 16 // chips

    def share(k, acc):
        for t in range(16):
            r, c = t // 2, t % 2
            u = t % tiles
            ar_s[k, t // tiles, 8 * u : 8 * u + 8, :] = acc[8 * r : 8 * r + 8, 128 * c : 128 * c + 128]

        def one(chip):
            pltpu.make_async_remote_copy(
                src_ref=ar_s.at[k, chip], dst_ref=ar_a.at[lat], send_sem=as_sem.at[0], recv_sem=ar_sem.at[0],
                device_id=(member, chip * 2 + k), device_id_type=MESH,
            ).start()

        def at(i, stay):
            y = wrap(my_y + ring(i, ny), ny)
            one((1 - my_x) * ny + y)
            if not stay:
                one(my_x * ny + y)

        around(ny, 0, ny, at)
        home = lat // 2

        @pl.when(my_core == k)
        def _():
            ar_a[lat] = ar_s[k, home]

        @pl.when(my_core != k)
        def _():
            one(home)

    def backward(jp, last=False):
        if jp < 2:
            even = jp * 8
            va = rg[0].astype(F32)[:, even : even + 8]
            vb = rg[1].astype(F32)[:, even : even + 8]
            one = jnp.where(low4, va, pltpu.roll(vb, 4, axis=1))
            two = jnp.where(low4, pltpu.roll(va, 4, axis=1), vb)
        else:
            block = rg[jp].astype(F32)
            one, two = block[:, :8], block[:, 8:]
        bs[:, :128] = one.reshape(cols, 128).astype(BF16)
        bs[:, 128:] = two.reshape(cols, 128).astype(BF16)

        def out_step(xc, inner):
            rows = pl.ds(pl.multiple_of(xc * XC, XC), XC)
            grad = dot(wave[rows, :], bs[...])
            grad16 = grad.astype(BF16)
            gfull[rows, :] = grad16
            turned = grad16.astype(F32).T.astype(BF16)
            total = jnp.zeros((64, 256), F32)
            for g in range(4):
                total = total + dot(turned[64 * g : 64 * g + 64], hid[jp, rows, 256 * g : 256 * g + 256])
            acc_out[...] += total
            return inner

        def in_step(xc, inner):
            rows = pl.ds(pl.multiple_of(xc * XC, XC), XC)
            act = (dot(gfull[rows, :], w_pull[...]) * slope[jp, rows, :].astype(F32)).astype(BF16)
            total = jnp.zeros((64, 256), F32)
            for g in range(4):
                total = total + dot(s_cx[jp, 64 * g : 64 * g + 64, rows], act[:, 256 * g : 256 * g + 256])
            acc_in[...] += total
            return inner

        lax.fori_loop(0, nlon // XC, out_step, 0)
        if last:
            share(0, acc_out)
        lax.fori_loop(0, nlon // XC, in_step, 0)

    here(0, rg, recv2)
    here(1, rg, recv2)
    left(1, 1, sg, send2)
    send_half(3, 0, *out2)
    backward(0)
    left(2, 0, sg, send2)
    send_half(3, 1, *out2)
    backward(1)
    wait_bytes(lrow1.at[pl.ds(0, nl - 1)], lr_sem.at[0])
    lsend2[...] = jnp.sum(lrow1[...], axis=0)
    to_members(lsend2, lrow2, ls_sem.at[1], lr_sem.at[1])
    lrow2[member] = lsend2[...]
    here(2, rg, recv2)
    backward(2)
    here(3, rg, recv2)
    backward(3, True)

    share(1, acc_in)
    wait_bytes(ar_a.at[pl.ds(0, nl - 1)], ar_sem.at[0])
    ar_p[...] = jnp.sum(ar_a[...], axis=0)
    to_members(ar_p, ar_b, as_sem.at[1], ar_sem.at[1])
    ar_b[member] = ar_p[...]
    wait_bytes(ar_b.at[pl.ds(0, nm - 1)], ar_sem.at[1])
    ar_q[...] = jnp.sum(ar_b[...], axis=0)
    to_lats(lambda t: ar_q, ar_c, as_sem.at[2], ar_sem.at[2])
    ar_c[lat] = ar_q[...]
    wait_bytes(lrow2.at[pl.ds(0, nm - 1)], lr_sem.at[1])
    out_loss[...] = jnp.sum(lrow2[...], axis=0)
    for t in range(4):
        for hf in range(2):
            if (t, hf) not in ((1, 0), (1, 1), (2, 0)):
                left(t, hf, sf, send1)
            if (t, hf) not in ((0, 0), (0, 1), (1, 0), (1, 1), (2, 0)):
                left(t, hf, sg, send2)
    wait_bytes(lrow1.at[pl.ds(0, nl - 1)], ls_sem.at[0])
    wait_bytes(lrow2.at[pl.ds(0, nm - 1)], ls_sem.at[1])
    wait_bytes(ar_a.at[pl.ds(0, nl - 1)], as_sem.at[0])
    wait_bytes(ar_b.at[pl.ds(0, nm - 1)], as_sem.at[1])
    wait_bytes(ar_c.at[pl.ds(0, nl - 1)], ar_sem.at[2])
    for k, out in ((0, out_out), (1, out_in)):
        for t in range(16):
            r, c = t // 2, t % 2
            u = t % tiles
            out[8 * r : 8 * r + 8, 128 * c : 128 * c + 128] = ar_c[2 * (t // tiles) + k, 8 * u : 8 * u + 8, :]
    wait_bytes(ar_c.at[pl.ds(0, nl - 1)], as_sem.at[2])


def finish(scale, g_in, g_out, loss, o_in, o_out, o_loss):
    o_in[...] = g_in[...]
    o_out[...] = g_out[...]
    o_loss[...] = jnp.sum(loss[...], axis=1, keepdims=True) * scale


def body(nm, nl, state, target, w_in, w_out, legendre, wavenumber_of):
    _, channels, hemis, rows, nlon = state.shape
    slots, deg, nj = legendre.shape
    waves = slots * nl
    cols = 2 * waves
    ng = 2 * nl
    base = jnp.asarray(base_table(nlon, waves))
    vmem = pl.BlockSpec(memory_space=pltpu.VMEM)
    hbm = pl.BlockSpec(memory_space=pl.ANY)
    dma = pltpu.SemaphoreType.DMA
    piece = 8 * (32 // nl)
    v = pltpu.VMEM
    sums = (
        jax.ShapeDtypeStruct((64, 256), F32),
        jax.ShapeDtypeStruct((64, 256), F32),
        jax.ShapeDtypeStruct((1, 128), F32),
    )
    parts = pl.pallas_call(
        functools.partial(kernel, nm, nl),
        out_shape=sums,
        in_specs=[hbm, hbm, vmem, vmem, hbm, hbm, vmem],
        out_specs=(vmem, vmem, vmem),
        scratch_shapes=[
            v((channels, hemis, rows, nlon), BF16),
            v((nlon // 128, channels * hemis * rows, 128), F32),
            v((4, 256, nlon), BF16),
            v((cols, nlon), BF16),
            v((cols, 128), F32),
            v((cols, nlon), BF16),
            v((nlon, cols), BF16),
            v((256, 1024), BF16),
            v((1024, 256), BF16),
            v((256, 1024), BF16),
            v((4, nlon, 1024), BF16),
            v((4, nlon, 1024), BF16),
            v((nlon, 256), BF16),
            v((nlon, 256), BF16),
            v((2, 2, ng, 8, 128), F32),
            v((4, ng, 16, 128), BF16),
            v((4, ng, 16, 128), BF16),
            v((ng, 32, 128), F32),
            v((2, ng, 16, 128), F32),
            v((ng, 32, 128), F32),
            v((2, ng, 16, 128), F32),
            v((4, ng, 16, 128), BF16),
            v((4, ng, 16, 128), BF16),
            v((4, deg, nj), BF16),
            v((4, deg, nj), BF16),
            v((4, nj, deg), BF16),
            v((2, channels, slots, deg), BF16),
            v((deg // 128, 2 * channels * slots, 128), F32),
            v((8, deg, 256), BF16),
            v((2, 2, deg, 256), F32),
            v((2, 2, deg, 256), BF16),
            v((cols, 256), BF16),
            v((64, 256), F32),
            v((64, 256), F32),
            v((1, 128), F32),
            v((nl, 1, 128), F32),
            v((1, 128), F32),
            v((nm, 1, 128), F32),
            v((2, nl // 2, piece, 128), F32),
            v((nl, piece, 128), F32),
            v((piece, 128), F32),
            v((nm, piece, 128), F32),
            v((piece, 128), F32),
            v((nl, piece, 128), F32),
            dma((4,)), dma((8,)), dma((4,)), dma((8,)), dma((4,)),
            dma((2,)), dma((2,)), dma((3,)), dma((3,)),
        ],
        compiler_params=pltpu.CompilerParams(
            collective_id=0, has_side_effects=True, vmem_limit_bytes=60 * 1024 * 1024
        ),
    )(state[0], target, w_in, w_out.T, legendre, base, wavenumber_of.reshape(-1, 128))
    scale = 0.5 / ((nm // 2) * channels) / (waves * deg)
    grad_in, grad_out, loss = pl.pallas_call(
        functools.partial(finish, scale),
        out_shape=(sums[0], sums[1], jax.ShapeDtypeStruct((1, 1), F32)),
        in_specs=[vmem, vmem, vmem],
        out_specs=(vmem, vmem, vmem),
    )(*parts)
    return loss.reshape(()), grad_in, grad_out.T


def solution(mesh):
    return jax.shard_map(
        functools.partial(body, mesh.shape["member"], mesh.shape["lat"]),
        mesh=mesh,
        in_specs=(
            P("member", None, None, "lat", None),
            P(None, None, "lat", None),
            P(),
            P(),
            P("lat", None, None),
            P(),
        ),
        out_specs=(P(), P(), P()),
        check_vma=False,
    )
```

```python
import functools
import math

import jax
import jax.numpy as jnp
import numpy as np
from jax import lax
from jax.experimental import pallas as pl
from jax.experimental.pallas import tpu as pltpu
from jax.sharding import PartitionSpec as P

MESH = pl.DeviceIdType.MESH
F32 = jnp.float32
BF16 = jnp.bfloat16
XC = 1024


def dot(a, b):
    return jnp.dot(a, b, preferred_element_type=F32)


def base_table(nlon, waves):
    cell = np.arange(nlon, dtype=np.int64)[None, :]
    wave = np.arange(waves, dtype=np.int64)[:, None]
    angle = (cell * wave % nlon).astype(np.float32) * np.float32(2.0 * math.pi / nlon)
    both = np.concatenate([np.cos(angle), -np.sin(angle)], axis=0) / np.float32(math.sqrt(nlon))
    return both.astype(jnp.bfloat16)


def kernel(
    nm, nl, state_hbm, target_hbm, w_in_ref, w_out_ref, leg_hbm, base_hbm, wn_ref,
    out_in, out_out, out_loss,
    st_raw, st32, s_cx, base, wcol, wave_t, wave, w_in_bd, w_out_bd, w_pull, hid, slope, fore, gfull,
    hold, sf, rf, rf_a, rf_b, fg_a, fg_b, sg, rg, leg, leg_p, leg_t, tgt, tw, tgt_t, acc32, gb, bs,
    acc_out, acc_in, lsend, lrow1, lsend2, lrow2, ar_s, ar_a, ar_p, ar_b, ar_q, ar_c,
    in_sem, send1, recv1, send2, recv2, ls_sem, lr_sem, as_sem, ar_sem,
):
    member = lax.axis_index("member")
    lat = lax.axis_index("lat")
    half = lax.rem(member, 2)
    base_member = member - half
    ng = 2 * nl
    me = half * nl + lat
    nlon = wave.shape[0]
    cols = wave.shape[1]
    waves = cols // 2
    deg = leg.shape[1]
    nj = leg.shape[2]

    ny, nz = nl // 4, nm // 2
    my_core, my_y, my_x, my_z = lax.rem(lat, 2), lax.rem(lat // 2, ny), lat // (2 * ny), member // 2
    members = (member, base_member + 1 - half)
    halves = (half, 1 - half)
    beside = [[x * 2 * ny + c for c in (my_core, 1 - my_core)] for x in (my_x, 1 - my_x)]

    def ring(i, size):
        return size // 2 + (1 - 2 * lax.rem(i, 2)) * ((i + 1) // 2)

    def wrap(v, size):
        return jnp.where(v >= size, v - size, v)

    def around(size, lo, hi, act):
        if hi > lo:
            lax.fori_loop(lo, min(hi, size - 1), lambda i, carry: (act(i, False), carry)[1], 0, unroll=True)
        if hi == size:
            act(size - 1, True)

    def group_step(act):
        def at(i, stay):
            y = wrap(my_y + ring(i, ny), ny) * 2
            for h in range(2):
                for x in range(2):
                    for c in range(2):
                        if not (stay and h == x == c == 0):
                            there = beside[x][c] + y
                            act((members[h], there), halves[h] * nl + there)

        return at

    def lat_step(act):
        def at(i, stay):
            y = wrap(my_y + ring(i, ny), ny) * 2
            for x in (1, 0):
                for c in range(2):
                    if not (stay and x == c == 0):
                        act(beside[x][c] + y)

        return at

    def member_step(act):
        def at(i, stay):
            z = wrap(my_z + ring(i, nz), nz) * 2
            for h in (1, 0):
                if not (stay and h == 0):
                    act(z + halves[h])

        return at

    c_state = pltpu.make_async_copy(state_hbm, st_raw, in_sem.at[0])
    c_base = pltpu.make_async_copy(base_hbm, base, in_sem.at[1])
    c_leg = pltpu.make_async_copy(leg_hbm.at[pl.ds(half * 4, 4)], leg, in_sem.at[2])
    c_tgt = pltpu.make_async_copy(target_hbm, tgt, in_sem.at[3])
    c_base.start()
    c_state.start()
    c_leg.start()
    c_tgt.start()

    barrier = pltpu.get_barrier_semaphore()

    def greet(there):
        pl.semaphore_signal(barrier, inc=1, device_id=there, device_id_type=MESH)

    around(ny, 0, ny, group_step(lambda there, t: greet(there)))
    for d in range(1, nz):
        for h in range(2):
            greet((wrap(my_z + d, nz) * 2 + h, lat))

    w_in_bd[...] = jnp.zeros_like(w_in_bd)
    w_pull[...] = jnp.zeros_like(w_pull)
    tall = w_out_ref[...].astype(F32)
    wide = jnp.concatenate([tall, tall, tall, tall], axis=0).T
    lane_group = lax.broadcasted_iota(jnp.int32, wide.shape, 1) >> 6
    for g in range(4):
        w_in_bd[64 * g : 64 * g + 64, 256 * g : 256 * g + 256] = w_in_ref[...]
        w_pull[64 * g : 64 * g + 64, 256 * g : 256 * g + 256] = w_out_ref[...]
        w_out_bd[256 * g : 256 * g + 256, :] = jnp.where(lane_group == g, wide, 0.0).astype(BF16)

    rows_of = [
        jnp.broadcast_to(wn_ref[r : r + 1, :].astype(F32), (128, 128)).T for r in range(wn_ref.shape[0])
    ]
    by_owner = jnp.concatenate(rows_of, axis=0).reshape(nl, 8, 128)
    sub = lax.broadcasted_iota(jnp.int32, (nl, 8, 128), 1)
    r2, r4, r6 = (pltpu.roll(by_owner, k, axis=1) for k in (2, 4, 6))
    first = jnp.where(sub < 2, by_owner, jnp.where(sub < 6, r2, r4))
    second = jnp.where(sub < 2, r4, jnp.where(sub < 6, r6, by_owner))
    wcol[: nl * 8] = first.reshape(nl * 8, 128)
    wcol[nl * 8 :] = second.reshape(nl * 8, 128)

    c_base.wait()
    lb = min(128, waves)
    rb = min(128, cols)

    def order_rows(r, carry):
        rows = pl.ds(pl.multiple_of(r * rb, rb), rb)
        number = wcol[rows, :][:, :lb]
        part = (lax.broadcasted_iota(jnp.int32, (rb, lb), 0) >> 1) & 1
        lane = lax.broadcasted_iota(jnp.int32, (rb, lb), 1)
        blocks = []
        for b in range(cols // lb):
            q, start = b * lb // waves, b * lb % waves
            same = number == (lane + start).astype(F32)
            blocks.append(jnp.where(same & (part == q), 1.0, 0.0))
        pick = jnp.concatenate(blocks, axis=1).astype(BF16)
        wave_t[rows, :] = dot(pick, base[...]).astype(BF16)
        return carry

    lax.fori_loop(0, cols // rb, order_rows, 0)

    c_state.wait()

    def widen(xt, carry):
        lanes = pl.ds(pl.multiple_of(xt * 128, 128), 128)
        st32[xt] = st_raw[:, :, :, lanes].astype(F32).reshape(st32.shape[1], 128)
        return carry

    lax.fori_loop(0, nlon // 128, widen, 0)

    spans = ((0, ny // 2), (ny // 2, ny))
    counts = (ng // 2, ng // 2 - 1)

    def send_half(tile, hf, src, dst, ssem, rsem):
        def one(there, t):
            pltpu.make_async_remote_copy(
                src_ref=src.at[tile, t], dst_ref=dst.at[tile, me],
                send_sem=ssem.at[2 * tile + hf], recv_sem=rsem.at[tile],
                device_id=there, device_id_type=MESH,
            ).start()

        around(ny, *spans[hf], group_step(one))

    def send_tile(tile, src, dst, ssem, rsem):
        send_half(tile, 0, src, dst, ssem, rsem)
        send_half(tile, 1, src, dst, ssem, rsem)
        dst[tile, me] = src[tile, me]

    def wait_bytes(ref, sem):
        pltpu.make_async_copy(ref, ref, sem).wait()

    def left(tile, hf, src, ssem):
        wait_bytes(src.at[tile, pl.ds(0, counts[hf])], ssem.at[2 * tile + hf])

    def here(tile, dst, rsem):
        wait_bytes(dst.at[tile, pl.ds(0, ng - 1)], rsem.at[tile])

    out1 = (sf, rf, send1, recv1)
    out2 = (sg, rg, send2, recv2)
    low4 = lax.broadcasted_iota(jnp.int32, (ng, 8, 128), 1) < 4

    def forward(jp, carry):
        def network(xc, inner):
            rows = pl.ds(pl.multiple_of(xc * XC, XC), XC)
            turned = []
            for xt in range(XC // 128):
                tile = xc * (XC // 128) + xt
                parts = [
                    st32[tile, pl.ds(h * 8 + jp * 2 + j2, 64, stride=16), :]
                    for j2 in range(2) for h in range(2)
                ]
                block = jnp.concatenate(parts, axis=0)
                s_cx[jp, :, pl.ds(pl.multiple_of(tile * 128, 128), 128)] = block.astype(BF16)
                turned.append(block.T)
            field = jnp.concatenate(turned, axis=0)
            pre = dot(field.astype(BF16), w_in_bd[...])
            sig = 0.5 + 0.5 * jnp.tanh(0.5 * pre)
            hidden = (pre * sig).astype(BF16)
            hid[jp, rows, :] = hidden
            slope[jp, rows, :] = (sig * (1.0 + pre * (1.0 - sig))).astype(BF16)
            fore[rows, :] = (field + dot(hidden, w_out_bd[...])).astype(BF16)
            return inner

        lax.fori_loop(0, nlon // XC, network, 0)
        modes = dot(wave_t[...], fore[...])
        one, two = modes[:, :128].reshape(ng, 8, 128), modes[:, 128:].reshape(ng, 8, 128)

        @pl.when(jp == 0)
        def _():
            pl.semaphore_wait(barrier, ng - 1 + nm - 2)

        @pl.when(jp < 2)
        def _():
            sf[jp] = jnp.concatenate([one, two], axis=1).astype(BF16)
            send_tile(jp, *out1)

        @pl.when(jp >= 2)
        def _():
            hold[jp - 2, 0] = jnp.where(low4, one, pltpu.roll(two, 4, axis=1))
            hold[jp - 2, 1] = jnp.where(low4, pltpu.roll(one, 4, axis=1), two)

        return carry

    lax.fori_loop(0, 4, forward, 0)
    for ig in range(2):
        sf[2 + ig] = jnp.concatenate([hold[0, ig], hold[1, ig]], axis=1).astype(BF16)
    send_tile(2, *out1)

    c_leg.wait()
    c_tgt.wait()
    col = lax.broadcasted_iota(jnp.int32, (nj, nj), 1)
    row = lax.broadcasted_iota(jnp.int32, (nj, nj), 0)
    from_col = jnp.where(col >= 4 * nl, col - 4 * nl, col)
    wanted = (from_col >> 2) * 8 + (from_col & 3) + jnp.where(col >= 4 * nl, 4, 0)
    perm = jnp.where(row == wanted, 1.0, 0.0).astype(BF16)
    for i in range(4):
        moved = dot(leg[i], perm)
        leg_p[i] = moved.astype(BF16)
        leg_t[i] = moved.T.astype(BF16)
    for b in range(deg // 128):
        tw[b] = tgt[:, :, :, 128 * b : 128 * b + 128].astype(F32).reshape(tw.shape[1], 128)
    for b in range(deg // 128):
        for i in range(8):
            parts = [tw[b, pl.ds(q * 512 + i, 64, stride=8), :] for q in (0, 0, 1, 1)]
            tgt_t[i, 128 * b : 128 * b + 128, :] = jnp.concatenate(parts, axis=0).T.astype(BF16)

    left(1, 0, sf, send1)
    left(1, 1, sf, send1)
    send_half(3, 0, *out1)
    rf[3, me] = sf[3, me]

    def turn_wave(xt, carry):
        start = pl.multiple_of(xt * 128, 128)
        wave[pl.ds(start, 128), :] = wave_t[:, pl.ds(start, 128)].astype(F32).T.astype(BF16)
        return carry

    lax.fori_loop(0, nlon // 128, turn_wave, 0)
    acc_out[...] = jnp.zeros_like(acc_out)
    acc_in[...] = jnp.zeros_like(acc_in)
    left(2, 0, sf, send1)
    send_half(3, 1, *out1)

    for t in range(2):
        here(t, rf, recv1)
        rf_a[:, 16 * t : 16 * t + 16, :] = rf[t].astype(F32)

    own = wcol[pl.ds(pl.multiple_of(me * 8, 8), 8), :].astype(jnp.int32)
    obj = 1.0 / ((nm // 2) * 64)
    nb = 128
    flat_a = rf_a.reshape(ng * 32, 128)
    flat_ga = fg_a.reshape(ng * 32, 128)

    def middle(ig, loss8):
        here(2 + ig, rf, recv1)
        rf_b[ig] = rf[2 + ig].astype(F32)
        flat_b = rf_b.at[ig].reshape(ng * 16, 128)
        flat_gb = fg_b.at[ig].reshape(ng * 16, 128)
        for i2 in range(2):
            for e in range(2):
                early = [
                    flat_a[pl.ds(e * nl * 32 + ig * 4 + q * 2 + i2, nl * 4, stride=8), :] for q in range(2)
                ]
                late = [flat_b[pl.ds(e * nl * 16 + q * 2 + i2, nl * 4, stride=4), :] for q in range(2)]
                modes = jnp.concatenate(
                    [jnp.concatenate(early, axis=1), jnp.concatenate(late, axis=1)], axis=0
                )
                acc32[i2, e] = dot(leg_p[2 * ig + i2], modes.astype(BF16))

        def compare(c, carry):
            rows = pl.ds(pl.multiple_of(c * nb, nb), nb)
            degree = lax.broadcasted_iota(jnp.int32, (nb, 128), 0) + c * nb
            south = lax.broadcasted_iota(jnp.int32, (nb, 128), 1) >= 64
            loss = jnp.zeros((nb, 128), F32)
            for i2 in range(2):
                gap = degree - own[4 * ig + i2 : 4 * ig + i2 + 1, :]
                live = gap >= 0
                sign = jnp.where((gap & 1) == 0, 1.0, -1.0)
                turn = jnp.where(south, sign, 1.0)
                for q in range(2):
                    lanes = slice(128 * q, 128 * q + 128)
                    coeffs = []
                    for e in range(2):
                        part = acc32[i2, e, rows, lanes]
                        whole = part + sign * pltpu.roll(part, 64, axis=1)
                        coeffs.append(jnp.where(live, whole, 0.0).astype(BF16).astype(F32))
                    aim = tgt_t[half * 4 + 2 * ig + i2, rows, lanes].astype(F32) * turn
                    d0, d1, ds = coeffs[0] - aim, coeffs[1] - aim, coeffs[0] - coeffs[1]
                    u0, u1, us = d0 * d0 + 1.0, d1 * d1 + 1.0, ds * ds + 1.0
                    r0, r1, rs = lax.rsqrt(u0), lax.rsqrt(u1), lax.rsqrt(us)
                    term = 0.5 * ((u0 * r0 - 1.0) + (u1 * r1 - 1.0) - (us * rs - 1.0))
                    loss = loss + jnp.where(live, term, 0.0)
                    pull = 0.5 * (ds * rs)
                    gb[i2, 0, rows, lanes] = jnp.where(live, (0.5 * (d0 * r0) - pull) * obj, 0.0).astype(BF16)
                    gb[i2, 1, rows, lanes] = jnp.where(live, (0.5 * (d1 * r1) + pull) * obj, 0.0).astype(BF16)
            return carry + jnp.sum(loss.reshape(nb // 8, 8, 128), axis=0)

        loss8 = lax.fori_loop(0, deg // nb, compare, loss8)
        for i2 in range(2):
            for e in range(2):
                back = dot(leg_t[2 * ig + i2], gb[i2, e])
                for q in range(2):
                    lanes = slice(128 * q, 128 * q + 128)
                    flat_gb[pl.ds(e * nl * 16 + q * 2 + i2, nl * 4, stride=4), :] = back[: nl * 4, lanes]
                    flat_ga[pl.ds(e * nl * 32 + ig * 4 + q * 2 + i2, nl * 4, stride=8), :] = back[nl * 4 :, lanes]
        sg[ig] = fg_b[ig].astype(BF16)
        send_tile(ig, *out2)
        return loss8

    loss8 = middle(0, jnp.zeros((8, 128), F32))
    loss8 = middle(1, loss8)
    for t in range(2):
        sg[2 + t] = fg_a[:, 16 * t : 16 * t + 16, :].astype(BF16)
        rg[2 + t, me] = sg[2 + t, me]

    def to_lats(src_of, dst, ssem, rsem):
        def one(t):
            pltpu.make_async_remote_copy(
                src_ref=src_of(t), dst_ref=dst.at[lat], send_sem=ssem, recv_sem=rsem,
                device_id=(member, t), device_id_type=MESH,
            ).start()

        around(ny, 0, ny, lat_step(one))

    def to_members(src, dst, ssem, rsem):
        def one(t):
            pltpu.make_async_remote_copy(
                src_ref=src, dst_ref=dst.at[member], send_sem=ssem, recv_sem=rsem,
                device_id=(t, lat), device_id_type=MESH,
            ).start()

        around(nz, 0, nz, member_step(one))

    lsend[...] = jnp.sum(loss8, axis=0, keepdims=True)
    to_lats(lambda t: lsend, lrow1, ls_sem.at[0], lr_sem.at[0])
    lrow1[lat] = lsend[...]

    left(0, 0, sg, send2)
    left(0, 1, sg, send2)
    send_half(2, 0, *out2)
    left(1, 0, sg, send2)
    send_half(2, 1, *out2)

    chips = nl // 2
    tiles = 16 // chips

    def share(k, acc):
        for t in range(16):
            r, c = t // 2, t % 2
            u = t % tiles
            ar_s[k, t // tiles, 8 * u : 8 * u + 8, :] = acc[8 * r : 8 * r + 8, 128 * c : 128 * c + 128]

        def one(chip):
            pltpu.make_async_remote_copy(
                src_ref=ar_s.at[k, chip], dst_ref=ar_a.at[lat], send_sem=as_sem.at[0], recv_sem=ar_sem.at[0],
                device_id=(member, chip * 2 + k), device_id_type=MESH,
            ).start()

        def at(i, stay):
            y = wrap(my_y + ring(i, ny), ny)
            one((1 - my_x) * ny + y)
            if not stay:
                one(my_x * ny + y)

        around(ny, 0, ny, at)
        home = lat // 2

        @pl.when(my_core == k)
        def _():
            ar_a[lat] = ar_s[k, home]

        @pl.when(my_core != k)
        def _():
            one(home)

    def backward(jp, last=False):
        if jp < 2:
            even = jp * 8
            va = rg[0].astype(F32)[:, even : even + 8]
            vb = rg[1].astype(F32)[:, even : even + 8]
            one = jnp.where(low4, va, pltpu.roll(vb, 4, axis=1))
            two = jnp.where(low4, pltpu.roll(va, 4, axis=1), vb)
        else:
            block = rg[jp].astype(F32)
            one, two = block[:, :8], block[:, 8:]
        bs[:, :128] = one.reshape(cols, 128).astype(BF16)
        bs[:, 128:] = two.reshape(cols, 128).astype(BF16)

        def out_step(xc, inner):
            rows = pl.ds(pl.multiple_of(xc * XC, XC), XC)
            grad = dot(wave[rows, :], bs[...])
            grad16 = grad.astype(BF16)
            gfull[rows, :] = grad16
            turned = grad16.astype(F32).T.astype(BF16)
            total = jnp.zeros((64, 256), F32)
            for g in range(4):
                total = total + dot(turned[64 * g : 64 * g + 64], hid[jp, rows, 256 * g : 256 * g + 256])
            acc_out[...] += total
            return inner

        def in_step(xc, inner):
            rows = pl.ds(pl.multiple_of(xc * XC, XC), XC)
            act = (dot(gfull[rows, :], w_pull[...]) * slope[jp, rows, :].astype(F32)).astype(BF16)
            total = jnp.zeros((64, 256), F32)
            for g in range(4):
                total = total + dot(s_cx[jp, 64 * g : 64 * g + 64, rows], act[:, 256 * g : 256 * g + 256])
            acc_in[...] += total
            return inner

        lax.fori_loop(0, nlon // XC, out_step, 0)
        if last:
            share(0, acc_out)
        lax.fori_loop(0, nlon // XC, in_step, 0)

    here(0, rg, recv2)
    here(1, rg, recv2)
    left(1, 1, sg, send2)
    send_half(3, 0, *out2)
    backward(0)
    left(2, 0, sg, send2)
    send_half(3, 1, *out2)
    backward(1)
    wait_bytes(lrow1.at[pl.ds(0, nl - 1)], lr_sem.at[0])
    lsend2[...] = jnp.sum(lrow1[...], axis=0)
    to_members(lsend2, lrow2, ls_sem.at[1], lr_sem.at[1])
    lrow2[member] = lsend2[...]
    here(2, rg, recv2)
    backward(2)
    here(3, rg, recv2)
    backward(3, True)

    share(1, acc_in)
    wait_bytes(ar_a.at[pl.ds(0, nl - 1)], ar_sem.at[0])
    ar_p[...] = jnp.sum(ar_a[...], axis=0)
    to_members(ar_p, ar_b, as_sem.at[1], ar_sem.at[1])
    ar_b[member] = ar_p[...]
    wait_bytes(ar_b.at[pl.ds(0, nm - 1)], ar_sem.at[1])
    ar_q[...] = jnp.sum(ar_b[...], axis=0)
    to_lats(lambda t: ar_q, ar_c, as_sem.at[2], ar_sem.at[2])
    ar_c[lat] = ar_q[...]
    wait_bytes(lrow2.at[pl.ds(0, nm - 1)], lr_sem.at[1])
    out_loss[...] = jnp.sum(lrow2[...], axis=0)
    for t in range(4):
        for hf in range(2):
            if (t, hf) not in ((1, 0), (1, 1), (2, 0)):
                left(t, hf, sf, send1)
            if (t, hf) not in ((0, 0), (0, 1), (1, 0), (1, 1), (2, 0)):
                left(t, hf, sg, send2)
    wait_bytes(lrow1.at[pl.ds(0, nl - 1)], ls_sem.at[0])
    wait_bytes(lrow2.at[pl.ds(0, nm - 1)], ls_sem.at[1])
    wait_bytes(ar_a.at[pl.ds(0, nl - 1)], as_sem.at[0])
    wait_bytes(ar_b.at[pl.ds(0, nm - 1)], as_sem.at[1])
    wait_bytes(ar_c.at[pl.ds(0, nl - 1)], ar_sem.at[2])
    for k, out in ((0, out_out), (1, out_in)):
        for t in range(16):
            r, c = t // 2, t % 2
            u = t % tiles
            out[8 * r : 8 * r + 8, 128 * c : 128 * c + 128] = ar_c[2 * (t // tiles) + k, 8 * u : 8 * u + 8, :]
    wait_bytes(ar_c.at[pl.ds(0, nl - 1)], as_sem.at[2])


def finish(scale, g_in, g_out, loss, o_in, o_out, o_loss):
    o_in[...] = g_in[...]
    o_out[...] = g_out[...]
    o_loss[...] = jnp.sum(loss[...], axis=1, keepdims=True) * scale


def body(nm, nl, state, target, w_in, w_out, legendre, wavenumber_of):
    _, channels, hemis, rows, nlon = state.shape
    slots, deg, nj = legendre.shape
    waves = slots * nl
    cols = 2 * waves
    ng = 2 * nl
    base = jnp.asarray(base_table(nlon, waves))
    vmem = pl.BlockSpec(memory_space=pltpu.VMEM)
    hbm = pl.BlockSpec(memory_space=pl.ANY)
    dma = pltpu.SemaphoreType.DMA
    piece = 8 * (32 // nl)
    v = pltpu.VMEM
    sums = (
        jax.ShapeDtypeStruct((64, 256), F32),
        jax.ShapeDtypeStruct((64, 256), F32),
        jax.ShapeDtypeStruct((1, 128), F32),
    )
    parts = pl.pallas_call(
        functools.partial(kernel, nm, nl),
        out_shape=sums,
        in_specs=[hbm, hbm, vmem, vmem, hbm, hbm, vmem],
        out_specs=(vmem, vmem, vmem),
        scratch_shapes=[
            v((channels, hemis, rows, nlon), BF16),
            v((nlon // 128, channels * hemis * rows, 128), F32),
            v((4, 256, nlon), BF16),
            v((cols, nlon), BF16),
            v((cols, 128), F32),
            v((cols, nlon), BF16),
            v((nlon, cols), BF16),
            v((256, 1024), BF16),
            v((1024, 256), BF16),
            v((256, 1024), BF16),
            v((4, nlon, 1024), BF16),
            v((4, nlon, 1024), BF16),
            v((nlon, 256), BF16),
            v((nlon, 256), BF16),
            v((2, 2, ng, 8, 128), F32),
            v((4, ng, 16, 128), BF16),
            v((4, ng, 16, 128), BF16),
            v((ng, 32, 128), F32),
            v((2, ng, 16, 128), F32),
            v((ng, 32, 128), F32),
            v((2, ng, 16, 128), F32),
            v((4, ng, 16, 128), BF16),
            v((4, ng, 16, 128), BF16),
            v((4, deg, nj), BF16),
            v((4, deg, nj), BF16),
            v((4, nj, deg), BF16),
            v((2, channels, slots, deg), BF16),
            v((deg // 128, 2 * channels * slots, 128), F32),
            v((8, deg, 256), BF16),
            v((2, 2, deg, 256), F32),
            v((2, 2, deg, 256), BF16),
            v((cols, 256), BF16),
            v((64, 256), F32),
            v((64, 256), F32),
            v((1, 128), F32),
            v((nl, 1, 128), F32),
            v((1, 128), F32),
            v((nm, 1, 128), F32),
            v((2, nl // 2, piece, 128), F32),
            v((nl, piece, 128), F32),
            v((piece, 128), F32),
            v((nm, piece, 128), F32),
            v((piece, 128), F32),
            v((nl, piece, 128), F32),
            dma((4,)), dma((8,)), dma((4,)), dma((8,)), dma((4,)),
            dma((2,)), dma((2,)), dma((3,)), dma((3,)),
        ],
        compiler_params=pltpu.CompilerParams(
            collective_id=0, has_side_effects=True, vmem_limit_bytes=60 * 1024 * 1024
        ),
    )(state[0], target, w_in, w_out.T, legendre, base, wavenumber_of.reshape(-1, 128))
    scale = 0.5 / ((nm // 2) * channels) / (waves * deg)
    grad_in, grad_out, loss = pl.pallas_call(
        functools.partial(finish, scale),
        out_shape=(sums[0], sums[1], jax.ShapeDtypeStruct((1, 1), F32)),
        in_specs=[vmem, vmem, vmem],
        out_specs=(vmem, vmem, vmem),
    )(*parts)
    return loss.reshape(()), grad_in, grad_out.T


def solution(mesh):
    return jax.shard_map(
        functools.partial(body, mesh.shape["member"], mesh.shape["lat"]),
        mesh=mesh,
        in_specs=(
            P("member", None, None, "lat", None),
            P(None, None, "lat", None),
            P(),
            P(),
            P("lat", None, None),
            P(),
        ),
        out_specs=(P(), P(), P()),
        check_vma=False,
    )
```
